128 devices in a mesh: pw: 16 (over z, x_lo, core), band: 8 (over y, x_hi).
Axes of the slice: x: 4 (x_hi: 2, x_lo: 2; x = x_hi * 2 + x_lo), y: 4, z: 4, core: 2. Of those that a mesh axis runs over, the one named last changes fastest.
Arguments:
- slab: bfloat16 [1024, 2, 196608], P('band', None, 'pw'), may hold values from -0.013671875 to 0.013671875
- panel: float32 [32, 2, 196608], P('band', None, 'pw'), may hold values from -6 to 6
- potential: float32 [128, 128, 128], P('pw'), may hold values from -2 to 2
- pw_slot: int32 [196608], P('pw'), may hold values from 0 to 32767, as said below
- columns: int32 [4096], P('pw'), may hold values from 0 to 16383, as said below
Outputs:
- ritz_blocks: float32 [1024, 128], P('band', 'pw')
The draws below stay inside these ranges and needn't reach their ends.
Inputs may be any that keep to these rules, and one draw needn't show every extreme that they name: Entry d * 256 + s is the grid column i1 * 128 + i2 of column slot s of index d of pw; all entries are distinct, and together they are the columns nearest the grid's third axis. `pw_slot`: the rows held by index d of pw are distinct values c * 128 + i3: the plane wave at third index i3 of column slot c of index d; within each device they are the cells of its columns nearest the grid's anchor.
All inputs are finite; a program needn't handle non-finite values.
Results may differ from the reference program's by a relative error of at most 0.0029.
Values may be sent and summed in bfloat16 or wider, within the bound.
No kernel may reach another device: no remote copies, remote signals or barrier semaphores. Data moves between devices by JAX's collectives and lax.ppermute only.
A program may use at most 128 MiB of HBM per device.

```python
import jax
import jax.numpy as jnp
from jax import lax

N1 = 128
N2 = 128
N3 = 128
PW_DEV = 12288
COL_DEV = 256
NPW = 196608
BANDS = 1024
PANEL = 32


def signed_index(index, length):
    return jnp.where(index < length // 2, index, index - length)


def sphere_map(key):
    blocks = NPW // PW_DEV
    total_cols = N1 * N2
    grid_cols = jnp.arange(total_cols, dtype=jnp.int32)
    first = signed_index(grid_cols // N2, N1)
    second = signed_index(grid_cols % N2, N2)
    ties = jax.random.permutation(jax.random.fold_in(key, 5), total_cols).astype(jnp.int32)
    ranks = (first * first + second * second) * total_cols + ties
    nearest = jnp.argsort(ranks, stable=True)[:COL_DEV * blocks].astype(jnp.int32)
    dealt = nearest.reshape(COL_DEV, blocks)[::-1].T
    slots = COL_DEV * N3
    slot_ids = jnp.arange(slots, dtype=jnp.int32)
    third = signed_index(slot_ids % N3, N3)

    def one_block(index):
        owned = dealt[index]
        holder = owned[slot_ids // N3]
        one = signed_index(holder // N2, N1)
        two = signed_index(holder % N2, N2)
        block_key = jax.random.fold_in(key, index + 100)
        block_ties = jax.random.permutation(jax.random.fold_in(block_key, 1), slots).astype(jnp.int32)
        block_ranks = (one * one + two * two + third * third) * slots + block_ties
        picked = jnp.argsort(block_ranks, stable=True)[:PW_DEV]
        shuffle = jax.random.permutation(jax.random.fold_in(block_key, 2), PW_DEV)
        return picked[shuffle].astype(jnp.int32)
    slot_rows = jax.vmap(one_block)(jnp.arange(blocks, dtype=jnp.int32)).reshape(-1)
    return (dealt.reshape(-1).astype(jnp.int32), slot_rows.astype(jnp.int32))


def draw_pw_slot(key, part):
    shared_cols, shared_slots = sphere_map(key)
    return shared_slots


def draw_columns(key, part):
    shared_cols, shared_slots = sphere_map(key)
    return shared_cols


def shard_levels(stream_key, extent, cuts, least, top_value):
    level = 1.0
    for position, parts in cuts:
        heights = jax.random.uniform(jax.random.fold_in(jax.random.fold_in(stream_key, 6), position), (parts,), jnp.float32, least / len(cuts), top_value / len(cuts))
        level = level * jnp.repeat(jnp.exp(heights), extent[position] // parts).reshape((-1,) + (1,) * (len(extent) - 1 - position))
    return level


def scatter_about(key, extent, width, most, pieces=(), held_as=jnp.bfloat16):
    drawn = jax.random.normal(key, extent, jnp.float32) * width
    if len(pieces) > 0:
        drawn = shard_levels(key, extent, pieces, -0.22, 0.18) * drawn
    return jnp.clip(drawn, min=-most, max=most).astype(held_as)


def setup_inputs(seed: int = 0) -> dict:
    arg_keys = jax.random.split(jax.random.key(seed), 6)
    return {
        "slab": scatter_about(arg_keys[0], (BANDS, 2, NPW), NPW ** -0.5, 0.013671875, ((0, 8), (2, 16))),
        "panel": scatter_about(arg_keys[1], (PANEL, 2, NPW), 1.0, 6.0, ((0, 8), (2, 16)), jnp.float32),
        "potential": jnp.clip(jax.random.uniform(arg_keys[2], (N3, N1, N2), jnp.float32, -2.0, 2.0) * shard_levels(arg_keys[2], (N3, N1, N2), ((0, 16),), -0.4, 0.0), -2.0, 2.0),
        "pw_slot": draw_pw_slot(jax.random.fold_in(arg_keys[5], 71), 0),
        "columns": draw_columns(jax.random.fold_in(arg_keys[5], 71), 0),
    }


def frequency(index, length):
    signed = jnp.where(index < length // 2, index, index - length)
    return signed.astype(jnp.float32) / (length / 2.0)


def kinetic_of(cells, first_len, second_len, third_len):
    first = cells // (second_len * third_len)
    second = (cells // third_len) % second_len
    third = cells % third_len
    fone = frequency(first, first_len)
    ftwo = frequency(second, second_len)
    fthree = frequency(third, third_len)
    return 0.5 * (fone * fone + ftwo * ftwo + fthree * fthree)


def make_kinds(pair):
    turned = jnp.stack([pair[:, 1], -pair[:, 0]], axis=1)
    return jnp.stack([pair, turned], axis=1)


def reference(slab, panel, potential, pw_slot, columns):
    owner = (jnp.arange(NPW, dtype=jnp.int32) // PW_DEV).astype(jnp.int32)
    column_index = (owner * COL_DEV + pw_slot // N3).astype(jnp.int32)
    pw_cell = (columns[column_index] * N3 + pw_slot % N3).astype(jnp.int32)
    kinetic = kinetic_of(pw_cell, N1, N2, N3)
    total = N1 * N2 * N3
    grid_potential = jnp.transpose(potential, (1, 2, 0))

    def apply_one(coeff_pair):
        real_part = jnp.zeros((total,), coeff_pair.dtype).at[pw_cell].set(coeff_pair[0])
        imag_part = jnp.zeros((total,), coeff_pair.dtype).at[pw_cell].set(coeff_pair[1])
        field = lax.complex(real_part, imag_part).reshape(N1, N2, N3)
        spread = jnp.fft.ifftn(field, norm="ortho")
        back = jnp.fft.fftn(grid_potential * spread, norm="ortho").reshape(-1)[pw_cell]
        return kinetic * coeff_pair + jnp.stack([jnp.real(back), jnp.imag(back)])

    applied = lax.map(apply_one, panel).astype(jnp.bfloat16)
    coeffs = panel.astype(jnp.bfloat16)
    operand = jnp.concatenate([make_kinds(applied), make_kinds(coeffs)], axis=1)
    operand = jnp.transpose(operand, (1, 0, 2, 3)).reshape(4 * PANEL, 2 * NPW)
    flat_slab = slab.reshape(BANDS, 2 * NPW)
    return jnp.dot(flat_slab, operand.T, preferred_element_type=jnp.float32)
```

```python
import functools
import math

import jax
import jax.numpy as jnp
import ml_dtypes
import numpy as np
from jax import lax
from jax.experimental import pallas as pl
from jax.experimental.pallas import tpu as pltpu
from jax.sharding import PartitionSpec as P

F32 = jnp.float32
BF16 = jnp.bfloat16
LEN = 128
HALF_THREE = 48
THIRDS = 2 * HALF_THREE
HALF_ONE = 40
FIRSTS = 2 * HALF_ONE
NT = (((1,), (1,)), ((), ()))


def split(table):
    high = table.astype(ml_dtypes.bfloat16)
    low = (table - high.astype(np.float64)).astype(ml_dtypes.bfloat16)
    return high, low


def rotation(outs, ins, sign):
    angles = sign * 2.0 * math.pi / LEN * ((outs[:, None] * ins[None, :]) % LEN)
    cosines = np.cos(angles) / math.sqrt(LEN)
    sines = np.sin(angles) / math.sqrt(LEN)
    return np.block([[cosines, -sines], [sines, cosines]])


@functools.lru_cache(None)
def tables(parts):
    grid = np.arange(LEN)
    thirds = np.arange(-HALF_THREE, HALF_THREE)
    row = np.arange(FIRSTS)
    firsts = 2 * (row % HALF_ONE) + row // HALF_ONE - HALF_ONE
    planes = LEN // parts
    order = np.arange(2 * LEN).reshape(2, parts, planes).transpose(1, 0, 2).ravel()
    return dict(
        three_in=split(rotation(grid, thirds, 1)[order]),
        three_out=split(rotation(thirds, grid, -1)[:, order]),
        two_in=split(rotation(grid, grid, 1).T),
        two_out=split(rotation(grid, grid, -1).T),
        one_in=split(rotation(grid, firsts, 1)),
        one_out=split(rotation(firsts, grid, -1)),
    )


def dot(a, b):
    return jnp.dot(a, b, preferred_element_type=F32)


def dot_nt(a, b):
    return lax.dot_general(a, b, NT, preferred_element_type=F32)


def halves(x):
    high = x.astype(BF16)
    return high, (x - high.astype(F32)).astype(BF16)


def one_hot(index, size):
    shape = (size, index.shape[1])
    return lax.broadcasted_iota(jnp.int32, shape, 0) == index


def third_slot(slot):
    return ((slot & (LEN - 1)) + HALF_THREE) & (LEN - 1)


def spread_kernel(slot_ref, panel_ref, high_ref, low_ref, out_ref, acc_ref):
    step = pl.program_id(0)
    cols = acc_ref.shape[1]

    @pl.when(step == 0)
    def _():
        acc_ref[...] = jnp.zeros_like(acc_ref)

    slot = slot_ref[...]
    pick = one_hot(slot >> 7, cols).astype(BF16)
    mask = one_hot(third_slot(slot), THIRDS)
    rows = []
    count = panel_ref.shape[0]
    for band in range(count):
        for part in range(2):
            high, low = halves(panel_ref[band, part : part + 1, :])
            for piece in (high, low):
                rows.append(jnp.where(mask, piece.astype(F32), 0.0).astype(BF16))
    acc_ref[...] += dot_nt(jnp.concatenate(rows, axis=0), pick)

    @pl.when(step == pl.num_programs(0) - 1)
    def _():
        owners = out_ref.shape[0]
        tall = out_ref.shape[1] // count
        for band in range(count):
            parts = [
                acc_ref[(4 * band + i) * THIRDS : (4 * band + i + 1) * THIRDS] for i in range(4)
            ]
            high = jnp.concatenate([parts[0], parts[2]], axis=0).astype(BF16)
            low = jnp.concatenate([parts[1], parts[3]], axis=0).astype(BF16)
            waves = dot(high_ref[...], high) + dot(low_ref[...], high) + dot(high_ref[...], low)
            out_ref[:, band * tall : (band + 1) * tall, :] = waves.astype(BF16).reshape(
                owners, tall, cols
            )


def spread(panel, slot, parts, cols, chunk):
    count, _, waves = panel.shape
    high, low = tables(parts)["three_in"]
    tall = 2 * LEN // parts
    whole = lambda *shape: pl.BlockSpec(shape, lambda i: (0,) * len(shape))
    return pl.pallas_call(
        spread_kernel,
        grid=(waves // chunk,),
        in_specs=[
            pl.BlockSpec((1, chunk), lambda i: (0, i)),
            pl.BlockSpec((count, 2, chunk), lambda i: (0, 0, i)),
            whole(*high.shape),
            whole(*low.shape),
        ],
        out_specs=whole(parts, count * tall, cols),
        out_shape=jax.ShapeDtypeStruct((parts, count * tall, cols), BF16),
        scratch_shapes=[pltpu.VMEM((4 * count * THIRDS, cols), F32)],
        compiler_params=pltpu.CompilerParams(vmem_limit_bytes=40 << 20),
        cost_estimate=pl.CostEstimate(
            flops=2 * 4 * count * THIRDS * cols * waves, bytes_accessed=4 << 20, transcendentals=0
        ),
        name="spread",
    )(slot, panel, jnp.asarray(high), jnp.asarray(low))


def grid_kernel(
    cols_ref, in_ref, pot_ref, ti_h, ti_l, oi_h, oi_l, oo_h, oo_l, to_h, to_l, out_ref, pick_ref, mask_ref, lhs_ref
):
    owners, tall, cols = in_ref.shape
    planes = tall // 2

    @pl.when(pl.program_id(0) == 0)
    def _():
        for owner in range(owners):
            here = slice(owner * cols, (owner + 1) * cols)
            column = cols_ref[owner : owner + 1, :]
            first = ((column >> 7) + HALF_ONE) & (LEN - 1)
            inner = (first & 1) * LEN + (column & (LEN - 1))
            pick_ref[:, here] = one_hot(inner, 2 * LEN).astype(BF16)
            mask_ref[:, here] = one_hot(first >> 1, HALF_ONE).astype(F32)

    for owner in range(owners):
        here = slice(owner * cols, (owner + 1) * cols)
        values = in_ref[owner].astype(F32)
        mask = mask_ref[:, here]
        lhs_ref[:, here] = jnp.concatenate(
            [values[row : row + 1] * mask for row in range(tall)], axis=0
        ).astype(BF16)
    field = dot_nt(lhs_ref[...], pick_ref[...]).astype(BF16)
    block = planes * HALF_ONE
    spun = []
    for low_bit in range(2):
        lanes = slice(low_bit * LEN, (low_bit + 1) * LEN)
        pair = jnp.concatenate([field[:block, lanes], field[block:, lanes]], axis=1)
        spun.append(dot(pair, ti_h[...]) + dot(pair, ti_l[...]))
    tower = jnp.concatenate(
        [
            jnp.concatenate(
                [
                    spun[low_bit][plane * HALF_ONE : (plane + 1) * HALF_ONE, part * LEN : (part + 1) * LEN]
                    for part in range(2)
                    for low_bit in range(2)
                ],
                axis=0,
            )
            for plane in range(planes)
        ],
        axis=1,
    )
    high, low = halves(tower)
    psi = dot(oi_h[...], high) + dot(oi_h[...], low) + dot(oi_l[...], high)
    pot = jnp.concatenate([pot_ref[plane] for plane in range(planes)], axis=1)
    psi = jnp.concatenate([psi[:LEN] * pot, psi[LEN:] * pot], axis=0)
    high, low = halves(psi)
    back = dot(oo_h[...], high) + dot(oo_h[...], low) + dot(oo_l[...], high)
    bent = []
    for low_bit in range(2):
        pair = jnp.concatenate(
            [
                jnp.concatenate(
                    [
                        back[
                            part * FIRSTS + low_bit * HALF_ONE : part * FIRSTS + (low_bit + 1) * HALF_ONE,
                            plane * LEN : (plane + 1) * LEN,
                        ]
                        for part in range(2)
                    ],
                    axis=1,
                )
                for plane in range(planes)
            ],
            axis=0,
        )
        high, low = halves(pair)
        bent.append(dot(high, to_h[...]) + dot(low, to_h[...]) + dot(high, to_l[...]))
    field = jnp.concatenate(
        [
            jnp.concatenate([bent[low_bit][:, part * LEN : (part + 1) * LEN] for low_bit in range(2)], axis=1)
            for part in range(2)
        ],
        axis=0,
    ).astype(BF16)
    for owner in range(owners):
        here = slice(owner * cols, (owner + 1) * cols)
        values = dot(field, pick_ref[:, here])
        mask = mask_ref[:, here]
        out_ref[owner] = jnp.concatenate(
            [
                jnp.sum(values[row * HALF_ONE : (row + 1) * HALF_ONE] * mask, axis=0, keepdims=True)
                for row in range(tall)
            ],
            axis=0,
        ).astype(BF16)


def on_grid(columns, waves, potential):
    owners, rows, cols = waves.shape
    planes = potential.shape[0]
    tall = 2 * planes
    count = rows // tall
    table = tables(owners)
    pieces = [jnp.asarray(t) for name in ("two_in", "one_in", "one_out", "two_out") for t in table[name]]
    whole = lambda *shape: pl.BlockSpec(shape, lambda i: (0,) * len(shape))
    return pl.pallas_call(
        grid_kernel,
        grid=(count,),
        in_specs=[
            whole(owners, cols),
            pl.BlockSpec((owners, tall, cols), lambda i: (0, i, 0)),
            whole(*potential.shape),
        ]
        + [whole(*piece.shape) for piece in pieces],
        out_specs=pl.BlockSpec((owners, tall, cols), lambda i: (0, i, 0)),
        out_shape=jax.ShapeDtypeStruct(waves.shape, BF16),
        scratch_shapes=[
            pltpu.VMEM((2 * LEN, owners * cols), BF16),
            pltpu.VMEM((HALF_ONE, owners * cols), F32),
            pltpu.VMEM((tall * HALF_ONE, owners * cols), BF16),
        ],
        compiler_params=pltpu.CompilerParams(vmem_limit_bytes=48 << 20),
        cost_estimate=pl.CostEstimate(
            flops=count * 2 * 2 * tall * HALF_ONE * 2 * LEN * owners * cols,
            bytes_accessed=4 << 20,
            transcendentals=0,
        ),
        name="on_grid",
    )(columns, waves, potential, *pieces)


def collect_kernel(slot_ref, cols_ref, panel_ref, in_ref, high_ref, low_ref, out_ref, held_ref):
    owners, rows, cols = in_ref.shape
    count = panel_ref.shape[0]
    tall = rows // count

    @pl.when(pl.program_id(0) == 0)
    def _():
        for band in range(count):
            waves = in_ref[:, band * tall : (band + 1) * tall, :].reshape(owners * tall, cols)
            found = dot(high_ref[...], waves) + dot(low_ref[...], waves)
            high, low = halves(found)
            held_ref[band * 2 * THIRDS : (band + 1) * 2 * THIRDS, :cols] = high
            held_ref[band * 2 * THIRDS : (band + 1) * 2 * THIRDS, cols:] = low
        column = cols_ref[...]
        first = column >> 7
        second = column & (LEN - 1)
        first = jnp.where(first < LEN // 2, first, first - LEN)
        second = jnp.where(second < LEN // 2, second, second - LEN)
        size = first * first + second * second
        line = lax.broadcasted_iota(jnp.int32, (16, cols), 0)
        size = jnp.where(line == 0, size >> 7, jnp.where(line == 1, size & (LEN - 1), 0))
        held_ref[2 * count * THIRDS :, :cols] = size.astype(F32).astype(BF16)
        held_ref[2 * count * THIRDS :, cols:] = jnp.zeros((16, cols), BF16)

    slot = slot_ref[...]
    pick = one_hot(slot >> 7, cols).astype(BF16)
    third = third_slot(slot)
    mask = one_hot(third, THIRDS).astype(F32)
    found = dot(held_ref[...], jnp.concatenate([pick, pick], axis=0))
    base = 2 * count * THIRDS
    third = (third - HALF_THREE).astype(F32)
    kinetic = (float(LEN) * found[base : base + 1] + found[base + 1 : base + 2] + third * third) * (
        2.0 / LEN**2
    )
    lines = []
    for band in range(count):
        for part in range(2):
            here = (2 * band + part) * THIRDS
            back = jnp.sum(found[here : here + THIRDS] * mask, axis=0, keepdims=True)
            lines.append(kinetic * panel_ref[band, part : part + 1, :] + back)
    out_ref[...] = jnp.concatenate(lines, axis=0).astype(BF16)


def collect(panel, slot, columns, waves, chunk):
    count, _, length = panel.shape
    owners, rows, cols = waves.shape
    high, low = tables(owners)["three_out"]
    whole = lambda *shape: pl.BlockSpec(shape, lambda i: (0,) * len(shape))
    return pl.pallas_call(
        collect_kernel,
        grid=(length // chunk,),
        in_specs=[
            pl.BlockSpec((1, chunk), lambda i: (0, i)),
            whole(1, cols),
            pl.BlockSpec((count, 2, chunk), lambda i: (0, 0, i)),
            whole(*waves.shape),
            whole(*high.shape),
            whole(*low.shape),
        ],
        out_specs=pl.BlockSpec((2 * count, chunk), lambda i: (0, i)),
        out_shape=jax.ShapeDtypeStruct((2 * count, length), BF16),
        scratch_shapes=[pltpu.VMEM((2 * count * THIRDS + 16, 2 * cols), BF16)],
        compiler_params=pltpu.CompilerParams(vmem_limit_bytes=40 << 20),
        cost_estimate=pl.CostEstimate(
            flops=2 * 4 * count * THIRDS * cols * length, bytes_accessed=4 << 20, transcendentals=0
        ),
        name="collect",
    )(slot, columns, panel, waves, jnp.asarray(high), jnp.asarray(low))


def project(piece, both):
    rows, length = piece.shape
    half = both.shape[0] // 2
    product = lax.dot_general(piece, both, NT, preferred_element_type=F32)
    product = product.reshape(rows // 2, 2, 2, half)
    real = product[:, 0, 0] + product[:, 1, 1]
    imag = product[:, 1, 0] - product[:, 0, 1]
    return jnp.concatenate([real, imag], axis=0)


def everywhere(x, axis):
    size = lax.axis_size(axis)
    copies = jnp.broadcast_to(x[None], (size,) + x.shape)
    return lax.all_to_all(copies, axis, split_axis=0, concat_axis=0, tiled=True)


def per_device(slab, panel, potential, pw_slot, columns):
    parts = lax.axis_size("pw")
    bands, _, length = slab.shape
    count = panel.shape[0]
    cols = columns.shape[0]
    slot = pw_slot.reshape(1, length)
    coeffs = lax.all_gather(panel.astype(BF16).reshape(2 * count, length), "band", axis=0, tiled=True)
    every_column = everywhere(columns, "pw")
    both = jnp.transpose(slab, (1, 0, 2)).reshape(2 * bands, length)
    waves = spread(panel, slot, parts, cols, 2048)
    waves = lax.all_to_all(waves, "pw", split_axis=0, concat_axis=0, tiled=True)
    waves = on_grid(every_column, waves, potential)
    waves = lax.all_to_all(waves, "pw", split_axis=0, concat_axis=0, tiled=True)
    applied = collect(panel, slot, columns.reshape(1, cols), waves, 2048)
    applied = everywhere(applied, "band").reshape(-1, length)
    terms = jnp.concatenate([project(applied, both), project(coeffs, both)], axis=0)
    terms = terms.reshape(parts, terms.shape[0] // parts, bands)
    terms = lax.all_to_all(terms, "pw", split_axis=0, concat_axis=0, tiled=True)
    return jnp.sum(terms, axis=0).T


def solution(mesh):
    in_specs = (P("band", None, "pw"), P("band", None, "pw"), P("pw", None, None), P("pw"), P("pw"))
    out_specs = P("band", "pw")
    return jax.shard_map(
        per_device, mesh=mesh, in_specs=in_specs, out_specs=out_specs, check_vma=False
    )
```

```python
import functools
import math

import jax
import jax.numpy as jnp
import ml_dtypes
import numpy as np
from jax import lax
from jax.experimental import pallas as pl
from jax.experimental.pallas import tpu as pltpu
from jax.sharding import PartitionSpec as P

F32 = jnp.float32
BF16 = jnp.bfloat16
LEN = 128
HALF_THREE = 44
THIRDS = 2 * HALF_THREE
HALF_ONE = 40
FIRSTS = 2 * HALF_ONE
NT = (((1,), (1,)), ((), ()))


def split(table):
    high = table.astype(ml_dtypes.bfloat16)
    low = (table - high.astype(np.float64)).astype(ml_dtypes.bfloat16)
    return high, low


def rotation(outs, ins, sign):
    angles = sign * 2.0 * math.pi / LEN * ((outs[:, None] * ins[None, :]) % LEN)
    cosines = np.cos(angles) / math.sqrt(LEN)
    sines = np.sin(angles) / math.sqrt(LEN)
    return np.block([[cosines, -sines], [sines, cosines]])


@functools.lru_cache(None)
def tables(parts):
    grid = np.arange(LEN)
    thirds = np.arange(-HALF_THREE, HALF_THREE)
    row = np.arange(FIRSTS)
    firsts = 2 * (row % HALF_ONE) + row // HALF_ONE - HALF_ONE
    planes = LEN // parts
    order = np.arange(2 * LEN).reshape(2, parts, planes).transpose(1, 0, 2).ravel()
    beside = lambda table, axis: np.concatenate(split(table), axis=axis)
    return dict(
        three_in=beside(rotation(grid, thirds, 1)[order], 0),
        three_out=beside(rotation(thirds, grid, -1)[:, order], 0),
        two_in=beside(rotation(grid, grid, 1).T, 1),
        two_out=beside(rotation(grid, grid, -1).T, 1),
        one_in=beside(rotation(grid, firsts, 1), 0),
        one_out=beside(rotation(firsts, grid, -1), 0),
    )


def dot(a, b):
    return jnp.dot(a, b, preferred_element_type=F32)


def dot_nt(a, b):
    return lax.dot_general(a, b, NT, preferred_element_type=F32)


def halves(x):
    high = x.astype(BF16)
    return high, (x - high.astype(F32)).astype(BF16)


def fold(x, axis):
    half = x.shape[axis] // 2
    return x[:half] + x[half:] if axis == 0 else x[:, :half] + x[:, half:]


def one_hot(index, size):
    shape = (size, index.shape[1])
    return lax.broadcasted_iota(jnp.int32, shape, 0) == index


def third_slot(slot):
    return ((slot & (LEN - 1)) + HALF_THREE) & (LEN - 1)


def whole(*shape):
    return pl.BlockSpec(shape, lambda *_: (0,) * len(shape))


def spread_kernel(slot_ref, cols_ref, panel_ref, table_ref, out_ref, coef_ref, acc_ref):
    step = pl.program_id(0)
    cols = cols_ref.shape[1]
    count = panel_ref.shape[0]
    spans = [slice(at, at + LEN) for at in range(0, cols, LEN)]

    @pl.when(step == 0)
    def _():
        acc_ref[...] = jnp.zeros_like(acc_ref)

    slot = slot_ref[...]
    pick = one_hot(slot >> 7, cols).astype(BF16)
    panel = jnp.concatenate([panel_ref[:, part, :] for part in range(2)], axis=0)
    high = panel.astype(BF16)
    coef_ref[...] = high
    wide = high.astype(F32)
    values = jnp.concatenate([wide, panel - wide], axis=0).astype(BF16)
    third = jnp.broadcast_to(third_slot(slot).astype(F32), values.shape).astype(BF16)
    zero = jnp.zeros_like(values)
    rows = jnp.concatenate(
        [jnp.where(third == jnp.asarray(index, BF16), values, zero) for index in range(THIRDS)], axis=0
    )
    found = dot_nt(rows, pick)
    for at, span in enumerate(spans):
        acc_ref[at] += found[:, span]

    @pl.when(step == pl.num_programs(0) - 1)
    def _():
        owners = out_ref.shape[0]
        tall = table_ref.shape[0] // 2 // owners
        line = lambda row: jnp.concatenate(
            [acc_ref[at, pl.ds(row, THIRDS, stride=4 * count), :] for at in range(len(spans))], axis=1
        )
        for band in range(count):
            high = jnp.concatenate([line(band), line(count + band)], axis=0).astype(BF16)
            low = jnp.concatenate([line(2 * count + band), line(3 * count + band)], axis=0).astype(BF16)
            waves = fold(dot(table_ref[...], high), 0) + dot(table_ref[: owners * tall], low)
            out_ref[:, band * tall : (band + 1) * tall, :] = waves.astype(BF16).reshape(
                owners, tall, cols
            )
        column = cols_ref[...]
        place = lax.broadcasted_iota(jnp.int32, (8, cols), 0)
        names = jnp.where(place == 0, column >> 7, jnp.where(place == 1, column & (LEN - 1), 0))
        names = names.astype(F32).astype(BF16)
        for owner in range(owners):
            out_ref[owner, count * tall :, :] = names


def spread(panel, slot, columns, parts, chunk):
    count, _, waves = panel.shape
    cols = columns.shape[1]
    table = tables(parts)["three_in"]
    tall = 2 * LEN // parts
    return pl.pallas_call(
        spread_kernel,
        grid=(waves // chunk,),
        in_specs=[
            pl.BlockSpec((1, chunk), lambda i: (0, i)),
            whole(1, cols),
            pl.BlockSpec((count, 2, chunk), lambda i: (0, 0, i)),
            whole(*table.shape),
        ],
        out_specs=[
            whole(parts, count * tall + 8, cols),
            pl.BlockSpec((2 * count, chunk), lambda i: (0, i)),
        ],
        out_shape=[
            jax.ShapeDtypeStruct((parts, count * tall + 8, cols), BF16),
            jax.ShapeDtypeStruct((2 * count, waves), BF16),
        ],
        scratch_shapes=[pltpu.VMEM((cols // LEN, 4 * count * THIRDS, LEN), F32)],
        compiler_params=pltpu.CompilerParams(vmem_limit_bytes=40 << 20),
        cost_estimate=pl.CostEstimate(
            flops=2 * 4 * count * THIRDS * cols * waves, bytes_accessed=4 << 20, transcendentals=0
        ),
        name="spread",
    )(slot, columns, panel, jnp.asarray(table))


def grid_kernel(in_ref, pot_ref, ti_ref, oi_ref, oo_ref, to_ref, out_ref, pick_ref, mask_ref, lhs_ref):
    owners, rows, cols = out_ref.shape
    planes = pot_ref.shape[0]
    tall = 2 * planes
    count = rows // tall

    for owner in range(owners):
        here = slice(owner * cols, (owner + 1) * cols)
        values = in_ref[owner].astype(F32)
        first = (values[rows : rows + 1].astype(jnp.int32) + HALF_ONE) & (LEN - 1)
        inner = (first & 1) * LEN + values[rows + 1 : rows + 2].astype(jnp.int32)
        pick_ref[:, here] = one_hot(inner, 2 * LEN).astype(BF16)
        mask = one_hot(first >> 1, HALF_ONE).astype(F32)
        mask_ref[:, here] = mask
        lhs_ref[:, here] = jnp.concatenate(
            [values[row : row + 1] * mask for row in range(rows)], axis=0
        ).astype(BF16)
    field = dot_nt(lhs_ref[...], pick_ref[...]).astype(BF16)
    block = planes * HALF_ONE
    lanes = lambda bit: slice(bit * LEN, (bit + 1) * LEN)
    spun = []
    for bit in range(2):
        pair = jnp.concatenate(
            [
                jnp.concatenate(
                    [field[(2 * band + part) * block : (2 * band + part + 1) * block, lanes(bit)] for part in range(2)],
                    axis=1,
                )
                for band in range(count)
            ],
            axis=0,
        )
        spun.append(fold(dot(pair, ti_ref[...]), 1))
    tower = jnp.concatenate(
        [
            jnp.concatenate(
                [
                    spun[bit][item * HALF_ONE : (item + 1) * HALF_ONE, lanes(part)]
                    for part in range(2)
                    for bit in range(2)
                ],
                axis=0,
            )
            for item in range(count * planes)
        ],
        axis=1,
    ).astype(BF16)
    psi = fold(dot(oi_ref[...], tower), 0)
    pot = jnp.concatenate([pot_ref[plane] for plane in range(planes)] * count, axis=1)
    psi = jnp.concatenate([psi[:LEN] * pot, psi[LEN:] * pot], axis=0).astype(BF16)
    back = fold(dot(oo_ref[...], psi), 0)
    bent = []
    for bit in range(2):
        pair = jnp.concatenate(
            [
                jnp.concatenate(
                    [
                        back[
                            part * FIRSTS + bit * HALF_ONE : part * FIRSTS + (bit + 1) * HALF_ONE,
                            item * LEN : (item + 1) * LEN,
                        ]
                        for part in range(2)
                    ],
                    axis=1,
                )
                for item in range(count * planes)
            ],
            axis=0,
        ).astype(BF16)
        bent.append(fold(dot(pair, to_ref[...]), 1))
    field = jnp.concatenate(
        [
            jnp.concatenate(
                [bent[bit][band * block : (band + 1) * block, lanes(part)] for bit in range(2)], axis=1
            )
            for band in range(count)
            for part in range(2)
        ],
        axis=0,
    ).astype(BF16)
    for owner in range(owners):
        here = slice(owner * cols, (owner + 1) * cols)
        values = dot(field, pick_ref[:, here])
        mask = mask_ref[:, here]
        out_ref[owner] = jnp.concatenate(
            [
                jnp.sum(values[row * HALF_ONE : (row + 1) * HALF_ONE] * mask, axis=0, keepdims=True)
                for row in range(rows)
            ],
            axis=0,
        ).astype(BF16)


def on_grid(waves, potential):
    owners, rows, cols = waves.shape
    rows -= 8
    pieces = [jnp.asarray(tables(owners)[name]) for name in ("two_in", "one_in", "one_out", "two_out")]
    return pl.pallas_call(
        grid_kernel,
        in_specs=[whole(*waves.shape), whole(*potential.shape)] + [whole(*piece.shape) for piece in pieces],
        out_specs=whole(owners, rows, cols),
        out_shape=jax.ShapeDtypeStruct((owners, rows, cols), BF16),
        scratch_shapes=[
            pltpu.VMEM((2 * LEN, owners * cols), BF16),
            pltpu.VMEM((HALF_ONE, owners * cols), F32),
            pltpu.VMEM((rows * HALF_ONE, owners * cols), BF16),
        ],
        compiler_params=pltpu.CompilerParams(vmem_limit_bytes=56 << 20),
        cost_estimate=pl.CostEstimate(
            flops=2 * 2 * rows * HALF_ONE * 2 * LEN * owners * cols,
            bytes_accessed=4 << 20,
            transcendentals=0,
        ),
        name="on_grid",
    )(waves, potential, *pieces)


def collect_kernel(slot_ref, cols_ref, panel_ref, in_ref, table_ref, out_ref, wide_ref, held_ref):
    owners, rows, cols = in_ref.shape
    count = panel_ref.shape[0]
    tall = rows // count
    base = 2 * count * THIRDS

    @pl.when(pl.program_id(0) == 0)
    def _():
        for band in range(count):
            waves = in_ref[:, band * tall : (band + 1) * tall, :].reshape(owners * tall, cols)
            found = fold(dot(table_ref[...], waves), 0)
            for part in range(2):
                for at in range(cols // LEN):
                    wide_ref[at, pl.ds(part * count + band, THIRDS, stride=2 * count), :] = found[
                        part * THIRDS : (part + 1) * THIRDS, at * LEN : (at + 1) * LEN
                    ]
        for at in range(cols // LEN):
            high, low = halves(wide_ref[at])
            held_ref[:base, at * LEN : (at + 1) * LEN] = high
            held_ref[:base, cols + at * LEN : cols + (at + 1) * LEN] = low
        column = cols_ref[...]
        first = column >> 7
        second = column & (LEN - 1)
        first = jnp.where(first < LEN // 2, first, first - LEN)
        second = jnp.where(second < LEN // 2, second, second - LEN)
        size = first * first + second * second
        line = lax.broadcasted_iota(jnp.int32, (16, cols), 0)
        size = jnp.where(line == 0, size >> 7, jnp.where(line == 1, size & (LEN - 1), 0))
        held_ref[base:, :cols] = size.astype(F32).astype(BF16)
        held_ref[base:, cols:] = jnp.zeros((16, cols), BF16)

    slot = slot_ref[...]
    pick = one_hot(slot >> 7, cols).astype(BF16)
    third = third_slot(slot)
    found = dot(held_ref[...], jnp.concatenate([pick, pick], axis=0))
    panel = jnp.concatenate([panel_ref[:, part, :] for part in range(2)], axis=0)
    where = jnp.broadcast_to(third, panel.shape)
    zero = jnp.zeros_like(panel)
    tall = 2 * count
    back = [zero] * 4
    for index in range(THIRDS):
        back[index % 4] += jnp.where(where == index, found[index * tall : (index + 1) * tall], zero)
    third = (third - HALF_THREE).astype(F32)
    kinetic = (float(LEN) * found[base : base + 1] + found[base + 1 : base + 2] + third * third) * (
        2.0 / LEN**2
    )
    out_ref[...] = (kinetic * panel + ((back[0] + back[1]) + (back[2] + back[3]))).astype(BF16)


def collect(panel, slot, columns, waves, start, length, chunk):
    count = panel.shape[0]
    owners, rows, cols = waves.shape
    table = tables(owners)["three_out"]
    skip = start // chunk
    return pl.pallas_call(
        collect_kernel,
        grid=(length // chunk,),
        in_specs=[
            pl.BlockSpec((1, chunk), lambda i: (0, i + skip)),
            whole(1, cols),
            pl.BlockSpec((count, 2, chunk), lambda i: (0, 0, i + skip)),
            whole(*waves.shape),
            whole(*table.shape),
        ],
        out_specs=pl.BlockSpec((2 * count, chunk), lambda i: (0, i)),
        out_shape=jax.ShapeDtypeStruct((2 * count, length), BF16),
        scratch_shapes=[
            pltpu.VMEM((cols // LEN, 2 * count * THIRDS, LEN), F32),
            pltpu.VMEM((2 * count * THIRDS + 16, 2 * cols), BF16),
        ],
        compiler_params=pltpu.CompilerParams(vmem_limit_bytes=40 << 20),
        cost_estimate=pl.CostEstimate(
            flops=2 * 4 * count * THIRDS * cols * length, bytes_accessed=4 << 20, transcendentals=0
        ),
        name="collect",
    )(slot, columns, panel, waves, jnp.asarray(table))


def project_kernel(sizes, seat_ref, *refs):
    pieces, (both_ref, prev_ref, out_ref, acc_ref) = refs[: len(sizes)], refs[len(sizes) :]
    step = pl.program_id(0)

    @pl.when(step == 0)
    def _():
        acc_ref[...] = jnp.zeros_like(acc_ref)

    rows = jnp.concatenate([ref[...].reshape(-1, ref.shape[-1]) for ref in pieces], axis=0)
    acc_ref[...] += dot_nt(rows, both_ref[...])

    @pl.when(step == pl.num_programs(0) - 1)
    def _():
        half = acc_ref.shape[1] // 2
        out_ref[...] = prev_ref[...]
        blocks = []
        for piece in range(acc_ref.shape[0] // 8):
            real = acc_ref[8 * piece : 8 * piece + 4]
            imag = acc_ref[8 * piece + 4 : 8 * piece + 8]
            blocks.append((real[:, :half] + imag[:, half:], imag[:, :half] - real[:, half:]))
        for pair in range(len(blocks) // 2):
            odd = seat_ref[8] == 1
            for part in range(2):
                one, two = blocks[2 * pair][part], blocks[2 * pair + 1][part]
                tile = jnp.concatenate([jnp.where(odd, two, one), jnp.where(odd, one, two)], axis=0)
                seat = seat_ref[pair] + part * (len(blocks) // 2)
                out_ref[seat] = out_ref[seat] + tile


def project(pieces, both, prev, seats, start, chunk):
    length = pieces[0].shape[-1]
    sizes = [math.prod(piece.shape[:-1]) for piece in pieces]
    skip = start // chunk
    block = lambda piece: pl.BlockSpec(
        piece.shape[:-1] + (chunk,), lambda i, *_, n=piece.ndim: (0,) * (n - 1) + (i,)
    )
    return pl.pallas_call(
        functools.partial(project_kernel, sizes),
        grid_spec=pltpu.PrefetchScalarGridSpec(
            num_scalar_prefetch=1,
            grid=(length // chunk,),
            in_specs=[block(piece) for piece in pieces]
            + [
                pl.BlockSpec((both.shape[0], chunk), lambda i, *_: (0, i + skip)),
                whole(*prev.shape),
            ],
            out_specs=whole(*prev.shape),
            scratch_shapes=[pltpu.VMEM((sum(sizes), both.shape[0]), F32)],
        ),
        out_shape=jax.ShapeDtypeStruct(prev.shape, F32),
        compiler_params=pltpu.CompilerParams(vmem_limit_bytes=32 << 20),
        cost_estimate=pl.CostEstimate(
            flops=2 * 256 * both.shape[0] * length,
            bytes_accessed=2 * both.shape[0] * length,
            transcendentals=0,
        ),
        name="project",
    )(seats, *pieces, both, prev)


def moved(x, axis, target):
    size = lax.axis_size(axis)
    return lax.ppermute(x, axis, [(i, target(i) % size) for i in range(size)])


def share(x):
    pair = jnp.stack([x, moved(x, "band", lambda i: i ^ 1)])
    below = moved(pair, "band", lambda i: i + 2)
    above = moved(pair, "band", lambda i: i - 2)
    far = [moved(below[0], "band", lambda i: i + 2), moved(above[1], "band", lambda i: i - 2)]
    return [pair, below, above] + far


def per_device(slab, panel, potential, pw_slot, columns):
    parts = lax.axis_size("pw")
    bands, _, length = slab.shape
    cols = columns.shape[0]
    slot = pw_slot.reshape(1, length)
    columns = columns.reshape(1, cols)
    waves, coeffs = spread(panel, slot, columns, parts, 2048)
    waves = lax.all_to_all(waves, "pw", split_axis=0, concat_axis=0, tiled=True)
    coeffs = lax.all_gather(coeffs, "band", axis=0, tiled=True)
    both = lax.optimization_barrier(jnp.transpose(slab, (1, 0, 2)).reshape(2 * bands, length))
    waves = on_grid(waves, potential)
    waves = lax.all_to_all(waves, "pw", split_axis=0, concat_axis=0, tiled=True)
    me = lax.axis_index("band")
    row, odd = me // 2, me % 2
    terms = jnp.zeros((parts, bands // parts, bands), F32)
    pick = lambda *seats: jnp.stack([jnp.asarray(seat, jnp.int32) for seat in seats])
    seats = pick(8, 9, 10, 11, 0, 0, 0, 0, 0)
    terms = project([coeffs], both, terms, seats, 0, 2048)
    seats = pick(row, (row + 3) % 4, (row + 1) % 4, (row + 2) % 4, 0, 0, 0, 0, odd)
    step = length // PIECES
    for piece in range(PIECES):
        applied = collect(panel, slot, columns, waves, piece * step, step, min(2048, step))
        terms = project(share(applied), both, terms, seats, piece * step, min(2048, step))
    terms = lax.all_to_all(terms, "pw", split_axis=0, concat_axis=0, tiled=True)
    return jnp.sum(terms, axis=0).T


PIECES = 2


def solution(mesh):
    in_specs = (P("band", None, "pw"), P("band", None, "pw"), P("pw", None, None), P("pw"), P("pw"))
    out_specs = P("band", "pw")
    return jax.shard_map(
        per_device, mesh=mesh, in_specs=in_specs, out_specs=out_specs, check_vma=False
    )
```

```python
import functools
import math

import jax
import jax.numpy as jnp
import ml_dtypes
import numpy as np
from jax import lax
from jax.experimental import pallas as pl
from jax.experimental.pallas import tpu as pltpu
from jax.sharding import PartitionSpec as P

F32 = jnp.float32
BF16 = jnp.bfloat16
LEN = 128
HALF_THREE = 44
THIRDS = 2 * HALF_THREE
EDGE = 40
PARTS = 4
STEP = 24
USED = 20
FIRSTS = PARTS * STEP
NT = (((1,), (1,)), ((), ()))


def split(table):
    high = table.astype(ml_dtypes.bfloat16)
    low = (table - high.astype(np.float64)).astype(ml_dtypes.bfloat16)
    return high, low


def rotation(outs, ins, sign):
    angles = sign * 2.0 * math.pi / LEN * ((outs[:, None] * ins[None, :]) % LEN)
    cosines = np.cos(angles) / math.sqrt(LEN)
    sines = np.sin(angles) / math.sqrt(LEN)
    return np.block([[cosines, -sines], [sines, cosines]])


@functools.lru_cache(None)
def tables(parts):
    grid = np.arange(LEN)
    thirds = np.arange(-HALF_THREE, HALF_THREE)
    row = np.arange(FIRSTS)
    firsts = PARTS * (row % STEP) + row // STEP - EDGE
    planes = LEN // parts
    order = np.arange(2 * LEN).reshape(2, parts, planes).transpose(1, 0, 2).ravel()
    beside = lambda table, axis: np.concatenate(split(table), axis=axis)
    return dict(
        three_in=beside(rotation(grid, thirds, 1)[order], 0),
        three_out=beside(rotation(thirds, grid, -1)[:, order], 0),
        two_in=beside(rotation(grid, grid, 1).T, 1),
        two_out=beside(rotation(grid, grid, -1).T, 1),
        one_in=beside(rotation(grid, firsts, 1), 0),
        one_out=beside(rotation(firsts, grid, -1), 0),
    )


def dot(a, b):
    return jnp.dot(a, b, preferred_element_type=F32)


def dot_nt(a, b):
    return lax.dot_general(a, b, NT, preferred_element_type=F32)


def halves(x):
    high = x.astype(BF16)
    return high, (x - high.astype(F32)).astype(BF16)


def fold(x, axis):
    half = x.shape[axis] // 2
    return x[:half] + x[half:] if axis == 0 else x[:, :half] + x[:, half:]


def one_hot(index, size):
    shape = (size, index.shape[1])
    return lax.broadcasted_iota(jnp.int32, shape, 0) == index


def third_slot(slot):
    return ((slot & (LEN - 1)) + HALF_THREE) & (LEN - 1)


def whole(*shape):
    return pl.BlockSpec(shape, lambda *_: (0,) * len(shape))


def spread_kernel(slot_ref, cols_ref, panel_ref, table_ref, out_ref, coef_ref, acc_ref):
    step = pl.program_id(0)
    cols = cols_ref.shape[1]
    count = panel_ref.shape[0]
    spans = [slice(at, at + LEN) for at in range(0, cols, LEN)]

    @pl.when(step == 0)
    def _():
        acc_ref[...] = jnp.zeros_like(acc_ref)

    slot = slot_ref[...]
    pick = one_hot(slot >> 7, cols).astype(BF16)
    panel = jnp.concatenate([panel_ref[:, part, :] for part in range(2)], axis=0)
    high = panel.astype(BF16)
    coef_ref[...] = high
    wide = high.astype(F32)
    values = jnp.concatenate([wide, panel - wide], axis=0).astype(BF16)
    third = jnp.broadcast_to(third_slot(slot).astype(F32), values.shape).astype(BF16)
    zero = jnp.zeros_like(values)
    rows = jnp.concatenate(
        [jnp.where(third == jnp.asarray(index, BF16), values, zero) for index in range(THIRDS)], axis=0
    )
    found = dot_nt(rows, pick)
    for at, span in enumerate(spans):
        acc_ref[at] += found[:, span]

    @pl.when(step == pl.num_programs(0) - 1)
    def _():
        owners = out_ref.shape[0]
        tall = table_ref.shape[0] // 2 // owners
        line = lambda row: jnp.concatenate(
            [acc_ref[at, pl.ds(row, THIRDS, stride=4 * count), :] for at in range(len(spans))], axis=1
        )
        for band in range(count):
            high = jnp.concatenate([line(band), line(count + band)], axis=0).astype(BF16)
            low = jnp.concatenate([line(2 * count + band), line(3 * count + band)], axis=0).astype(BF16)
            waves = fold(dot(table_ref[...], high), 0) + dot(table_ref[: owners * tall], low)
            out_ref[:, band * tall : (band + 1) * tall, :] = waves.astype(BF16).reshape(
                owners, tall, cols
            )
        column = cols_ref[...]
        place = lax.broadcasted_iota(jnp.int32, (8, cols), 0)
        names = jnp.where(place == 0, column >> 7, jnp.where(place == 1, column & (LEN - 1), 0))
        names = names.astype(F32).astype(BF16)
        for owner in range(owners):
            out_ref[owner, count * tall :, :] = names


def spread(panel, slot, columns, parts, chunk):
    count, _, waves = panel.shape
    cols = columns.shape[1]
    table = tables(parts)["three_in"]
    tall = 2 * LEN // parts
    return pl.pallas_call(
        spread_kernel,
        grid=(waves // chunk,),
        in_specs=[
            pl.BlockSpec((1, chunk), lambda i: (0, i)),
            whole(1, cols),
            pl.BlockSpec((count, 2, chunk), lambda i: (0, 0, i)),
            whole(*table.shape),
        ],
        out_specs=[
            whole(parts, count * tall + 8, cols),
            pl.BlockSpec((2 * count, chunk), lambda i: (0, i)),
        ],
        out_shape=[
            jax.ShapeDtypeStruct((parts, count * tall + 8, cols), BF16),
            jax.ShapeDtypeStruct((2 * count, waves), BF16),
        ],
        scratch_shapes=[pltpu.VMEM((cols // LEN, 4 * count * THIRDS, LEN), F32)],
        compiler_params=pltpu.CompilerParams(vmem_limit_bytes=56 << 20),
        cost_estimate=pl.CostEstimate(
            flops=2 * 4 * count * THIRDS * cols * waves, bytes_accessed=4 << 20, transcendentals=0
        ),
        name="spread",
    )(slot, columns, panel, jnp.asarray(table))


def grid_kernel(in_ref, pot_ref, ti_ref, oi_ref, oo_ref, to_ref, out_ref, pick_ref, first_ref, lhs_ref, found_ref, field_ref):
    owners, rows, cols = out_ref.shape
    planes = pot_ref.shape[0]
    tall = 2 * planes
    count = rows // tall

    for owner in range(owners):
        here = slice(owner * cols, (owner + 1) * cols)
        values = in_ref[owner].astype(F32)
        first = (values[rows : rows + 1].astype(jnp.int32) + EDGE) & (LEN - 1)
        inner = (first & (PARTS - 1)) * LEN + values[rows + 1 : rows + 2].astype(jnp.int32)
        pick_ref[:, here] = one_hot(inner, PARTS * LEN).astype(BF16)
        mask = one_hot(first // PARTS, STEP).astype(F32)
        first_ref[owner : owner + 1, :] = first // PARTS
        lhs_ref[:, here] = jnp.concatenate(
            [values[row : row + 1] * mask for row in range(rows)], axis=0
        ).astype(BF16)
    field = dot_nt(lhs_ref[...], pick_ref[...]).astype(BF16)
    block = planes * STEP
    lanes = lambda bit: slice(bit * LEN, (bit + 1) * LEN)
    spun = []
    for bit in range(PARTS):
        pair = jnp.concatenate(
            [
                jnp.concatenate(
                    [field[(2 * band + part) * block : (2 * band + part + 1) * block, lanes(bit)] for part in range(2)],
                    axis=1,
                )
                for band in range(count)
            ],
            axis=0,
        )
        spun.append(fold(dot(pair, ti_ref[...]), 1))
    tower = jnp.concatenate(
        [
            jnp.concatenate(
                [
                    spun[bit][item * STEP : (item + 1) * STEP, lanes(part)]
                    for part in range(2)
                    for bit in range(PARTS)
                ],
                axis=0,
            )
            for item in range(count * planes)
        ],
        axis=1,
    ).astype(BF16)
    psi = fold(dot(oi_ref[...], tower), 0)
    pot = jnp.concatenate([pot_ref[plane] for plane in range(planes)] * count, axis=1)
    psi = jnp.concatenate([psi[:LEN] * pot, psi[LEN:] * pot], axis=0).astype(BF16)
    back = fold(dot(oo_ref[...], psi), 0)
    bent = []
    for bit in range(PARTS):
        pair = jnp.concatenate(
            [
                jnp.concatenate(
                    [
                        back[
                            part * FIRSTS + bit * STEP : part * FIRSTS + (bit + 1) * STEP,
                            item * LEN : (item + 1) * LEN,
                        ]
                        for part in range(2)
                    ],
                    axis=1,
                )
                for item in range(count * planes)
            ],
            axis=0,
        ).astype(BF16)
        bent.append(fold(dot(pair, to_ref[...]), 1))
    for bit in range(PARTS):
        for item in range(count * planes):
            band, plane = divmod(item, planes)
            for part in range(2):
                found_ref[bit, pl.ds((2 * band + part) * planes + plane, USED, stride=rows), :] = bent[bit][
                    item * STEP : item * STEP + USED, lanes(part)
                ]
    for bit in range(PARTS):
        field_ref[:, lanes(bit)] = found_ref[bit].astype(BF16)
    for owner in range(owners):
        here = slice(owner * cols, (owner + 1) * cols)
        values = dot(field_ref[...], pick_ref[:, here])
        first = jnp.broadcast_to(first_ref[owner : owner + 1, :], (rows, cols))
        zero = jnp.zeros((rows, cols), F32)
        total = zero
        for at in range(USED):
            total += jnp.where(first == at, values[at * rows : (at + 1) * rows], zero)
        out_ref[owner] = total.astype(BF16)


def on_grid(waves, potential):
    owners, rows, cols = waves.shape
    rows -= 8
    pieces = [jnp.asarray(tables(owners)[name]) for name in ("two_in", "one_in", "one_out", "two_out")]
    return pl.pallas_call(
        grid_kernel,
        in_specs=[whole(*waves.shape), whole(*potential.shape)] + [whole(*piece.shape) for piece in pieces],
        out_specs=whole(owners, rows, cols),
        out_shape=jax.ShapeDtypeStruct((owners, rows, cols), BF16),
        scratch_shapes=[
            pltpu.VMEM((PARTS * LEN, owners * cols), BF16),
            pltpu.VMEM((owners, cols), jnp.int32),
            pltpu.VMEM((rows * STEP, owners * cols), BF16),
            pltpu.VMEM((PARTS, rows * USED, LEN), F32),
            pltpu.VMEM((rows * USED, PARTS * LEN), BF16),
        ],
        compiler_params=pltpu.CompilerParams(vmem_limit_bytes=56 << 20),
        cost_estimate=pl.CostEstimate(
            flops=2 * 2 * rows * USED * PARTS * LEN * owners * cols,
            bytes_accessed=4 << 20,
            transcendentals=0,
        ),
        name="on_grid",
    )(waves, potential, *pieces)


def collect_kernel(slot_ref, cols_ref, panel_ref, in_ref, table_ref, out_ref, wide_ref, held_ref):
    owners, rows, cols = in_ref.shape
    count = panel_ref.shape[0]
    tall = rows // count
    base = 2 * count * THIRDS

    @pl.when(pl.program_id(0) == 0)
    def _():
        for band in range(count):
            waves = in_ref[:, band * tall : (band + 1) * tall, :].reshape(owners * tall, cols)
            found = fold(dot(table_ref[...], waves), 0)
            for part in range(2):
                for at in range(cols // LEN):
                    wide_ref[at, pl.ds(part * count + band, THIRDS, stride=2 * count), :] = found[
                        part * THIRDS : (part + 1) * THIRDS, at * LEN : (at + 1) * LEN
                    ]
        for at in range(cols // LEN):
            high, low = halves(wide_ref[at])
            held_ref[:base, at * LEN : (at + 1) * LEN] = high
            held_ref[:base, cols + at * LEN : cols + (at + 1) * LEN] = low
        column = cols_ref[...]
        first = column >> 7
        second = column & (LEN - 1)
        first = jnp.where(first < LEN // 2, first, first - LEN)
        second = jnp.where(second < LEN // 2, second, second - LEN)
        size = first * first + second * second
        line = lax.broadcasted_iota(jnp.int32, (16, cols), 0)
        size = jnp.where(line == 0, size >> 7, jnp.where(line == 1, size & (LEN - 1), 0))
        held_ref[base:, :cols] = size.astype(F32).astype(BF16)
        held_ref[base:, cols:] = jnp.zeros((16, cols), BF16)

    slot = slot_ref[...]
    pick = one_hot(slot >> 7, cols).astype(BF16)
    third = third_slot(slot)
    found = dot(held_ref[...], jnp.concatenate([pick, pick], axis=0))
    panel = jnp.concatenate([panel_ref[:, part, :] for part in range(2)], axis=0)
    where = jnp.broadcast_to(third, panel.shape)
    zero = jnp.zeros_like(panel)
    tall = 2 * count
    back = [zero] * 4
    for index in range(THIRDS):
        back[index % 4] += jnp.where(where == index, found[index * tall : (index + 1) * tall], zero)
    third = (third - HALF_THREE).astype(F32)
    kinetic = (float(LEN) * found[base : base + 1] + found[base + 1 : base + 2] + third * third) * (
        2.0 / LEN**2
    )
    out_ref[...] = (kinetic * panel + ((back[0] + back[1]) + (back[2] + back[3]))).astype(BF16)


def collect(panel, slot, columns, waves, start, length, chunk):
    count = panel.shape[0]
    owners, rows, cols = waves.shape
    table = tables(owners)["three_out"]
    skip = start // chunk
    return pl.pallas_call(
        collect_kernel,
        grid=(length // chunk,),
        in_specs=[
            pl.BlockSpec((1, chunk), lambda i: (0, i + skip)),
            whole(1, cols),
            pl.BlockSpec((count, 2, chunk), lambda i: (0, 0, i + skip)),
            whole(*waves.shape),
            whole(*table.shape),
        ],
        out_specs=pl.BlockSpec((2 * count, chunk), lambda i: (0, i)),
        out_shape=jax.ShapeDtypeStruct((2 * count, length), BF16),
        scratch_shapes=[
            pltpu.VMEM((cols // LEN, 2 * count * THIRDS, LEN), F32),
            pltpu.VMEM((2 * count * THIRDS + 16, 2 * cols), BF16),
        ],
        compiler_params=pltpu.CompilerParams(vmem_limit_bytes=56 << 20),
        cost_estimate=pl.CostEstimate(
            flops=2 * 4 * count * THIRDS * cols * length, bytes_accessed=4 << 20, transcendentals=0
        ),
        name="collect",
    )(slot, columns, panel, waves, jnp.asarray(table))


def project_kernel(sizes, seat_ref, *refs):
    pieces, (both_ref, prev_ref, out_ref, acc_ref) = refs[: len(sizes)], refs[len(sizes) :]
    step = pl.program_id(0)

    @pl.when(step == 0)
    def _():
        acc_ref[...] = jnp.zeros_like(acc_ref)

    rows = jnp.concatenate([ref[...].reshape(-1, ref.shape[-1]) for ref in pieces], axis=0)
    acc_ref[...] += dot_nt(rows, both_ref[...])

    @pl.when(step == pl.num_programs(0) - 1)
    def _():
        half = acc_ref.shape[1] // 2
        out_ref[...] = prev_ref[...]
        blocks = []
        for piece in range(acc_ref.shape[0] // 8):
            real = acc_ref[8 * piece : 8 * piece + 4]
            imag = acc_ref[8 * piece + 4 : 8 * piece + 8]
            blocks.append((real[:, :half] + imag[:, half:], imag[:, :half] - real[:, half:]))
        for pair in range(len(blocks) // 2):
            odd = seat_ref[8] == 1
            for part in range(2):
                one, two = blocks[2 * pair][part], blocks[2 * pair + 1][part]
                tile = jnp.concatenate([jnp.where(odd, two, one), jnp.where(odd, one, two)], axis=0)
                seat = seat_ref[pair] + part * (len(blocks) // 2)
                out_ref[seat] = out_ref[seat] + tile


def project(pieces, both, prev, seats, start, chunk):
    length = pieces[0].shape[-1]
    sizes = [math.prod(piece.shape[:-1]) for piece in pieces]
    skip = start // chunk
    block = lambda piece: pl.BlockSpec(
        piece.shape[:-1] + (chunk,), lambda i, *_, n=piece.ndim: (0,) * (n - 1) + (i,)
    )
    return pl.pallas_call(
        functools.partial(project_kernel, sizes),
        grid_spec=pltpu.PrefetchScalarGridSpec(
            num_scalar_prefetch=1,
            grid=(length // chunk,),
            in_specs=[block(piece) for piece in pieces]
            + [
                pl.BlockSpec((both.shape[0], chunk), lambda i, *_: (0, i + skip)),
                whole(*prev.shape),
            ],
            out_specs=whole(*prev.shape),
            scratch_shapes=[pltpu.VMEM((sum(sizes), both.shape[0]), F32)],
        ),
        out_shape=jax.ShapeDtypeStruct(prev.shape, F32),
        compiler_params=pltpu.CompilerParams(vmem_limit_bytes=56 << 20),
        cost_estimate=pl.CostEstimate(
            flops=2 * 256 * both.shape[0] * length,
            bytes_accessed=2 * both.shape[0] * length,
            transcendentals=0,
        ),
        name="project",
    )(seats, *pieces, both, prev)


def moved(x, axis, target):
    size = lax.axis_size(axis)
    return lax.ppermute(x, axis, [(i, target(i) % size) for i in range(size)])


def share(x):
    pair = jnp.stack([x, moved(x, "band", lambda i: i ^ 1)])
    below = moved(pair, "band", lambda i: i + 2)
    above = moved(pair, "band", lambda i: i - 2)
    far = [moved(below[0], "band", lambda i: i + 2), moved(above[1], "band", lambda i: i - 2)]
    return [pair, below, above] + far


def per_device(slab, panel, potential, pw_slot, columns):
    parts = lax.axis_size("pw")
    bands, _, length = slab.shape
    cols = columns.shape[0]
    slot = pw_slot.reshape(1, length)
    columns = columns.reshape(1, cols)
    waves, coeffs = spread(panel, slot, columns, parts, 3072)
    waves = lax.all_to_all(waves, "pw", split_axis=0, concat_axis=0, tiled=True)
    coeffs = lax.all_gather(coeffs, "band", axis=0, tiled=True)
    both = jnp.transpose(slab, (1, 0, 2)).reshape(2 * bands, length)
    waves, both = lax.optimization_barrier((waves, both))
    waves = on_grid(waves, potential)
    waves = lax.all_to_all(waves, "pw", split_axis=0, concat_axis=0, tiled=True)
    waves, coeffs = lax.optimization_barrier((waves, coeffs))
    me = lax.axis_index("band")
    row, odd = me // 2, me % 2
    terms = jnp.zeros((parts, bands // parts, bands), F32)
    pick = lambda *seats: jnp.stack([jnp.asarray(seat, jnp.int32) for seat in seats])
    seats = pick(8, 9, 10, 11, 0, 0, 0, 0, 0)
    terms = project([coeffs], both, terms, seats, 0, 3072)
    seats = pick(row, (row + 3) % 4, (row + 1) % 4, (row + 2) % 4, 0, 0, 0, 0, odd)
    step = length // PIECES
    for piece in range(PIECES):
        applied = collect(panel, slot, columns, waves, piece * step, step, min(3072, step))
        terms = project(share(applied), both, terms, seats, piece * step, min(3072, step))
    terms = lax.all_to_all(terms, "pw", split_axis=0, concat_axis=0, tiled=True)
    return jnp.sum(terms, axis=0).T


PIECES = 2


def solution(mesh):
    in_specs = (P("band", None, "pw"), P("band", None, "pw"), P("pw", None, None), P("pw"), P("pw"))
    out_specs = P("band", "pw")
    return jax.shard_map(
        per_device, mesh=mesh, in_specs=in_specs, out_specs=out_specs, check_vma=False
    )
```

```python
import functools
import math

import jax
import jax.numpy as jnp
import ml_dtypes
import numpy as np
from jax import lax
from jax.experimental import pallas as pl
from jax.experimental.pallas import tpu as pltpu
from jax.sharding import PartitionSpec as P

F32 = jnp.float32
BF16 = jnp.bfloat16
LEN = 128
HALF_THREE = 44
THIRDS = 2 * HALF_THREE
EDGE = 40
PARTS = 4
STEP = 24
USED = 20
FIRSTS = PARTS * STEP
NT = (((1,), (1,)), ((), ()))


def split(table):
    high = table.astype(ml_dtypes.bfloat16)
    low = (table - high.astype(np.float64)).astype(ml_dtypes.bfloat16)
    return high, low


def rotation(outs, ins, sign):
    angles = sign * 2.0 * math.pi / LEN * ((outs[:, None] * ins[None, :]) % LEN)
    cosines = np.cos(angles) / math.sqrt(LEN)
    sines = np.sin(angles) / math.sqrt(LEN)
    return np.block([[cosines, -sines], [sines, cosines]])


@functools.lru_cache(None)
def tables(parts):
    grid = np.arange(LEN)
    thirds = np.arange(-HALF_THREE, HALF_THREE)
    row = np.arange(FIRSTS)
    firsts = PARTS * (row % STEP) + row // STEP - EDGE
    planes = LEN // parts
    order = np.arange(2 * LEN).reshape(2, parts, planes).transpose(1, 0, 2).ravel()
    beside = lambda table, axis: np.concatenate(split(table), axis=axis)
    return dict(
        three_in=beside(rotation(grid, thirds, 1)[order], 0),
        three_out=beside(rotation(thirds, grid, -1)[:, order], 0),
        two_in=beside(rotation(grid, grid, 1).T, 1),
        two_out=beside(rotation(grid, grid, -1).T, 1),
        one_in=beside(rotation(grid, firsts, 1), 0),
        one_out=beside(rotation(firsts, grid, -1), 0),
    )


def dot(a, b):
    return jnp.dot(a, b, preferred_element_type=F32)


def dot_nt(a, b):
    return lax.dot_general(a, b, NT, preferred_element_type=F32)


def halves(x):
    high = x.astype(BF16)
    return high, (x - high.astype(F32)).astype(BF16)


def fold(x, axis):
    half = x.shape[axis] // 2
    return x[:half] + x[half:] if axis == 0 else x[:, :half] + x[:, half:]


def one_hot(index, size):
    shape = (size, index.shape[1])
    return lax.broadcasted_iota(jnp.int32, shape, 0) == index


def third_slot(slot):
    return ((slot & (LEN - 1)) + HALF_THREE) & (LEN - 1)


def whole(*shape):
    return pl.BlockSpec(shape, lambda *_: (0,) * len(shape))


def spread_kernel(slot_ref, cols_ref, panel_ref, table_ref, out_ref, coef_ref, acc_ref):
    step = pl.program_id(0)
    cols = cols_ref.shape[1]
    count = panel_ref.shape[0]
    spans = [slice(at, at + LEN) for at in range(0, cols, LEN)]

    @pl.when(step == 0)
    def _():
        acc_ref[...] = jnp.zeros_like(acc_ref)

    slot = slot_ref[...]
    pick = one_hot(slot >> 7, cols).astype(BF16)
    panel = jnp.concatenate([panel_ref[:, part, :] for part in range(2)], axis=0)
    high = panel.astype(BF16)
    coef_ref[...] = high
    wide = high.astype(F32)
    values = jnp.concatenate([wide, panel - wide], axis=0).astype(BF16)
    third = jnp.broadcast_to(third_slot(slot).astype(F32), values.shape).astype(BF16)
    zero = jnp.zeros_like(values)
    rows = jnp.concatenate(
        [jnp.where(third == jnp.asarray(index, BF16), values, zero) for index in range(THIRDS)], axis=0
    )
    found = dot_nt(rows, pick)
    for at, span in enumerate(spans):
        acc_ref[at] += found[:, span]

    @pl.when(step == pl.num_programs(0) - 1)
    def _():
        owners = out_ref.shape[0]
        tall = table_ref.shape[0] // 2 // owners
        line = lambda row: jnp.concatenate(
            [acc_ref[at, pl.ds(row, THIRDS, stride=4 * count), :] for at in range(len(spans))], axis=1
        )
        for band in range(count):
            high = jnp.concatenate([line(band), line(count + band)], axis=0).astype(BF16)
            low = jnp.concatenate([line(2 * count + band), line(3 * count + band)], axis=0).astype(BF16)
            waves = fold(dot(table_ref[...], high), 0) + dot(table_ref[: owners * tall], low)
            out_ref[:, band * tall : (band + 1) * tall, :] = waves.astype(BF16).reshape(
                owners, tall, cols
            )
        column = cols_ref[...]
        place = lax.broadcasted_iota(jnp.int32, (8, cols), 0)
        names = jnp.where(place == 0, column >> 7, jnp.where(place == 1, column & (LEN - 1), 0))
        names = names.astype(F32).astype(BF16)
        for owner in range(owners):
            out_ref[owner, count * tall :, :] = names


def spread(panel, slot, columns, parts, chunk):
    count, _, waves = panel.shape
    cols = columns.shape[1]
    table = tables(parts)["three_in"]
    tall = 2 * LEN // parts
    return pl.pallas_call(
        spread_kernel,
        grid=(waves // chunk,),
        in_specs=[
            pl.BlockSpec((1, chunk), lambda i: (0, i)),
            whole(1, cols),
            pl.BlockSpec((count, 2, chunk), lambda i: (0, 0, i)),
            whole(*table.shape),
        ],
        out_specs=[
            whole(parts, count * tall + 8, cols),
            pl.BlockSpec((2 * count, chunk), lambda i: (0, i)),
        ],
        out_shape=[
            jax.ShapeDtypeStruct((parts, count * tall + 8, cols), BF16),
            jax.ShapeDtypeStruct((2 * count, waves), BF16),
        ],
        scratch_shapes=[pltpu.VMEM((cols // LEN, 4 * count * THIRDS, LEN), F32)],
        compiler_params=pltpu.CompilerParams(vmem_limit_bytes=56 << 20),
        cost_estimate=pl.CostEstimate(
            flops=2 * 4 * count * THIRDS * cols * waves, bytes_accessed=4 << 20, transcendentals=0
        ),
        name="spread",
    )(slot, columns, panel, jnp.asarray(table))


def grid_kernel(in_ref, pot_ref, ti_ref, oi_ref, oo_ref, to_ref, out_ref, pick_ref, first_ref, lhs_ref, found_ref, field_ref):
    owners, rows, cols = out_ref.shape
    planes = pot_ref.shape[0]
    tall = 2 * planes
    count = rows // tall

    for owner in range(owners):
        here = slice(owner * cols, (owner + 1) * cols)
        values = in_ref[owner].astype(F32)
        first = (values[rows : rows + 1].astype(jnp.int32) + EDGE) & (LEN - 1)
        inner = (first & (PARTS - 1)) * LEN + values[rows + 1 : rows + 2].astype(jnp.int32)
        pick_ref[:, here] = one_hot(inner, PARTS * LEN).astype(BF16)
        mask = one_hot(first // PARTS, STEP).astype(F32)
        first_ref[owner : owner + 1, :] = first // PARTS
        lhs_ref[:, here] = jnp.concatenate(
            [values[row : row + 1] * mask for row in range(rows)], axis=0
        ).astype(BF16)
    field = dot_nt(lhs_ref[...], pick_ref[...]).astype(BF16)
    block = planes * STEP
    lanes = lambda bit: slice(bit * LEN, (bit + 1) * LEN)
    spun = []
    for bit in range(PARTS):
        pair = jnp.concatenate(
            [
                jnp.concatenate(
                    [field[(2 * band + part) * block : (2 * band + part + 1) * block, lanes(bit)] for part in range(2)],
                    axis=1,
                )
                for band in range(count)
            ],
            axis=0,
        )
        spun.append(fold(dot(pair, ti_ref[...]), 1))
    tower = jnp.concatenate(
        [
            jnp.concatenate(
                [
                    spun[bit][item * STEP : (item + 1) * STEP, lanes(part)]
                    for part in range(2)
                    for bit in range(PARTS)
                ],
                axis=0,
            )
            for item in range(count * planes)
        ],
        axis=1,
    ).astype(BF16)
    psi = fold(dot(oi_ref[...], tower), 0)
    pot = jnp.concatenate([pot_ref[plane] for plane in range(planes)] * count, axis=1)
    psi = jnp.concatenate([psi[:LEN] * pot, psi[LEN:] * pot], axis=0).astype(BF16)
    back = fold(dot(oo_ref[...], psi), 0)
    bent = []
    for bit in range(PARTS):
        pair = jnp.concatenate(
            [
                jnp.concatenate(
                    [
                        back[
                            part * FIRSTS + bit * STEP : part * FIRSTS + (bit + 1) * STEP,
                            item * LEN : (item + 1) * LEN,
                        ]
                        for part in range(2)
                    ],
                    axis=1,
                )
                for item in range(count * planes)
            ],
            axis=0,
        ).astype(BF16)
        bent.append(fold(dot(pair, to_ref[...]), 1))
    for bit in range(PARTS):
        for item in range(count * planes):
            band, plane = divmod(item, planes)
            for part in range(2):
                found_ref[bit, pl.ds((2 * band + part) * planes + plane, USED, stride=rows), :] = bent[bit][
                    item * STEP : item * STEP + USED, lanes(part)
                ]
    for bit in range(PARTS):
        field_ref[:, lanes(bit)] = found_ref[bit].astype(BF16)
    for owner in range(owners):
        here = slice(owner * cols, (owner + 1) * cols)
        values = dot(field_ref[...], pick_ref[:, here])
        first = jnp.broadcast_to(first_ref[owner : owner + 1, :], (rows, cols))
        zero = jnp.zeros((rows, cols), F32)
        total = zero
        for at in range(USED):
            total += jnp.where(first == at, values[at * rows : (at + 1) * rows], zero)
        out_ref[owner] = total.astype(BF16)


def on_grid(waves, potential):
    owners, rows, cols = waves.shape
    rows -= 8
    pieces = [jnp.asarray(tables(owners)[name]) for name in ("two_in", "one_in", "one_out", "two_out")]
    return pl.pallas_call(
        grid_kernel,
        in_specs=[whole(*waves.shape), whole(*potential.shape)] + [whole(*piece.shape) for piece in pieces],
        out_specs=whole(owners, rows, cols),
        out_shape=jax.ShapeDtypeStruct((owners, rows, cols), BF16),
        scratch_shapes=[
            pltpu.VMEM((PARTS * LEN, owners * cols), BF16),
            pltpu.VMEM((owners, cols), jnp.int32),
            pltpu.VMEM((rows * STEP, owners * cols), BF16),
            pltpu.VMEM((PARTS, rows * USED, LEN), F32),
            pltpu.VMEM((rows * USED, PARTS * LEN), BF16),
        ],
        compiler_params=pltpu.CompilerParams(vmem_limit_bytes=56 << 20),
        cost_estimate=pl.CostEstimate(
            flops=2 * 2 * rows * USED * PARTS * LEN * owners * cols,
            bytes_accessed=4 << 20,
            transcendentals=0,
        ),
        name="on_grid",
    )(waves, potential, *pieces)


def collect_kernel(slot_ref, cols_ref, panel_ref, in_ref, table_ref, out_ref, wide_ref, held_ref):
    owners, rows, cols = in_ref.shape
    count = panel_ref.shape[0]
    tall = rows // count
    base = 2 * count * THIRDS

    @pl.when(pl.program_id(0) == 0)
    def _():
        for band in range(count):
            waves = in_ref[:, band * tall : (band + 1) * tall, :].reshape(owners * tall, cols)
            found = fold(dot(table_ref[...], waves), 0)
            for part in range(2):
                for at in range(cols // LEN):
                    wide_ref[at, pl.ds(part * count + band, THIRDS, stride=2 * count), :] = found[
                        part * THIRDS : (part + 1) * THIRDS, at * LEN : (at + 1) * LEN
                    ]
        for at in range(cols // LEN):
            high, low = halves(wide_ref[at])
            held_ref[:base, at * LEN : (at + 1) * LEN] = high
            held_ref[:base, cols + at * LEN : cols + (at + 1) * LEN] = low
        column = cols_ref[...]
        first = column >> 7
        second = column & (LEN - 1)
        first = jnp.where(first < LEN // 2, first, first - LEN)
        second = jnp.where(second < LEN // 2, second, second - LEN)
        size = first * first + second * second
        line = lax.broadcasted_iota(jnp.int32, (16, cols), 0)
        size = jnp.where(line == 0, size >> 7, jnp.where(line == 1, size & (LEN - 1), 0))
        held_ref[base:, :cols] = size.astype(F32).astype(BF16)
        held_ref[base:, cols:] = jnp.zeros((16, cols), BF16)

    slot = slot_ref[...]
    pick = one_hot(slot >> 7, cols).astype(BF16)
    third = third_slot(slot)
    found = dot(held_ref[...], jnp.concatenate([pick, pick], axis=0))
    panel = jnp.concatenate([panel_ref[:, part, :] for part in range(2)], axis=0)
    where = jnp.broadcast_to(third, panel.shape)
    zero = jnp.zeros_like(panel)
    tall = 2 * count
    back = [zero] * 4
    for index in range(THIRDS):
        back[index % 4] += jnp.where(where == index, found[index * tall : (index + 1) * tall], zero)
    third = (third - HALF_THREE).astype(F32)
    kinetic = (float(LEN) * found[base : base + 1] + found[base + 1 : base + 2] + third * third) * (
        2.0 / LEN**2
    )
    out_ref[...] = (kinetic * panel + ((back[0] + back[1]) + (back[2] + back[3]))).astype(BF16)


def collect(panel, slot, columns, waves, start, length, chunk):
    count = panel.shape[0]
    owners, rows, cols = waves.shape
    table = tables(owners)["three_out"]
    skip = start // chunk
    return pl.pallas_call(
        collect_kernel,
        grid=(length // chunk,),
        in_specs=[
            pl.BlockSpec((1, chunk), lambda i: (0, i + skip)),
            whole(1, cols),
            pl.BlockSpec((count, 2, chunk), lambda i: (0, 0, i + skip)),
            whole(*waves.shape),
            whole(*table.shape),
        ],
        out_specs=pl.BlockSpec((2 * count, chunk), lambda i: (0, i)),
        out_shape=jax.ShapeDtypeStruct((2 * count, length), BF16),
        scratch_shapes=[
            pltpu.VMEM((cols // LEN, 2 * count * THIRDS, LEN), F32),
            pltpu.VMEM((2 * count * THIRDS + 16, 2 * cols), BF16),
        ],
        compiler_params=pltpu.CompilerParams(vmem_limit_bytes=40 << 20),
        cost_estimate=pl.CostEstimate(
            flops=2 * 4 * count * THIRDS * cols * length, bytes_accessed=4 << 20, transcendentals=0
        ),
        name="collect",
    )(slot, columns, panel, waves, jnp.asarray(table))


def project_kernel(seat_ref, *refs):
    pieces, (both_ref, prev_ref, out_ref, acc_ref) = refs[:-4], refs[-4:]
    step = pl.program_id(0)

    @pl.when(step == 0)
    def _():
        acc_ref[...] = jnp.zeros_like(acc_ref)

    rows = jnp.concatenate([ref[...].reshape(-1, ref.shape[-1]) for ref in pieces], axis=0)
    acc_ref[...] += dot_nt(rows, both_ref[...])

    @pl.when(step == pl.num_programs(0) - 1)
    def _():
        total = acc_ref[...]
        half = total.shape[1] // 2
        pairs = total.shape[0] // 16
        odd = seat_ref[pairs] == 1
        out_ref[...] = prev_ref[...]
        for pair in range(pairs):
            mine = []
            for piece in (2 * pair, 2 * pair + 1):
                real = total[8 * piece : 8 * piece + 4]
                imag = total[8 * piece + 4 : 8 * piece + 8]
                mine.append((real[:, :half] + imag[:, half:], imag[:, :half] - real[:, half:]))
            for part in range(2):
                one, two = mine[0][part], mine[1][part]
                if pair < pairs // 2:
                    one, two = jnp.where(odd, two, one), jnp.where(odd, one, two)
                seat = seat_ref[pair] + part * (pairs // 2)
                out_ref[seat] = out_ref[seat] + jnp.concatenate([one, two], axis=0)


def project(pieces, coeffs, both, prev, seats, start, chunk):
    length = pieces[0].shape[-1]
    rows = sum(math.prod(piece.shape[:-1]) for piece in pieces) + coeffs.shape[0]
    skip = start // chunk
    block = lambda piece: pl.BlockSpec(
        piece.shape[:-1] + (chunk,), lambda i, *_, n=piece.ndim: (0,) * (n - 1) + (i,)
    )
    later = lambda wide: pl.BlockSpec((wide.shape[0], chunk), lambda i, *_: (0, i + skip))
    return pl.pallas_call(
        project_kernel,
        grid_spec=pltpu.PrefetchScalarGridSpec(
            num_scalar_prefetch=1,
            grid=(length // chunk,),
            in_specs=[block(piece) for piece in pieces] + [later(coeffs), later(both), whole(*prev.shape)],
            out_specs=whole(*prev.shape),
            scratch_shapes=[pltpu.VMEM((rows, both.shape[0]), F32)],
        ),
        out_shape=jax.ShapeDtypeStruct(prev.shape, F32),
        compiler_params=pltpu.CompilerParams(vmem_limit_bytes=56 << 20),
        cost_estimate=pl.CostEstimate(
            flops=2 * 256 * both.shape[0] * length,
            bytes_accessed=2 * both.shape[0] * length,
            transcendentals=0,
        ),
        name="project",
    )(seats, *pieces, coeffs, both, prev)


def moved(x, axis, target):
    size = lax.axis_size(axis)
    return lax.ppermute(x, axis, [(i, target(i) % size) for i in range(size)])


def share(x, terms):
    pair = jnp.stack([x, moved(x, "band", lambda i: i ^ 1)])
    below = moved(pair, "band", lambda i: i + 2)
    above = moved(pair, "band", lambda i: i - 2)
    first, second, terms = lax.optimization_barrier((below[0], above[1], terms))
    far = [moved(first, "band", lambda i: i + 2), moved(second, "band", lambda i: i - 2)]
    return [pair, below, above] + far, terms


def per_device(slab, panel, potential, pw_slot, columns):
    parts = lax.axis_size("pw")
    bands, _, length = slab.shape
    cols = columns.shape[0]
    slot = pw_slot.reshape(1, length)
    columns = columns.reshape(1, cols)
    waves, coeffs = spread(panel, slot, columns, parts, 3072)
    waves = lax.all_to_all(waves, "pw", split_axis=0, concat_axis=0, tiled=True)
    coeffs = lax.all_gather(coeffs, "band", axis=0, tiled=True)
    both = jnp.transpose(slab, (1, 0, 2)).reshape(2 * bands, length)
    waves, both = lax.optimization_barrier((waves, both))
    waves = on_grid(waves, potential)
    waves = lax.all_to_all(waves, "pw", split_axis=0, concat_axis=0, tiled=True)
    waves, coeffs = lax.optimization_barrier((waves, coeffs))
    me = lax.axis_index("band")
    row, odd = me // 2, me % 2
    terms = jnp.zeros((parts, bands // parts, bands), F32)
    pick = lambda *seats: jnp.stack([jnp.asarray(seat, jnp.int32) for seat in seats])
    seats = pick(row, (row + 3) % 4, (row + 1) % 4, (row + 2) % 4, 8, 9, 10, 11, odd)
    step = length // PIECES
    applied = [
        collect(panel, slot, columns, waves, piece * step, step, min(3072, step)) for piece in range(PIECES)
    ]
    for piece in range(PIECES):
        shared, terms = share(applied[piece], terms)
        terms = project(shared, coeffs, both, terms, seats, piece * step, min(CHUNK, step))
    terms = lax.all_to_all(terms, "pw", split_axis=0, concat_axis=0, tiled=True)
    return jnp.sum(terms, axis=0).T


PIECES = 2
CHUNK = 3072


def solution(mesh):
    in_specs = (P("band", None, "pw"), P("band", None, "pw"), P("pw", None, None), P("pw"), P("pw"))
    out_specs = P("band", "pw")
    return jax.shard_map(
        per_device, mesh=mesh, in_specs=in_specs, out_specs=out_specs, check_vma=False
    )
```

```python
import functools
import math

import jax
import jax.numpy as jnp
import ml_dtypes
import numpy as np
from jax import lax
from jax.experimental import pallas as pl
from jax.experimental.pallas import tpu as pltpu
from jax.sharding import PartitionSpec as P

F32 = jnp.float32
BF16 = jnp.bfloat16
LEN = 128
HALF_THREE = 44
THIRDS = 2 * HALF_THREE
EDGE = 40
PARTS = 4
STEP = 24
USED = 20
FIRSTS = PARTS * STEP
NT = (((1,), (1,)), ((), ()))


def split(table):
    high = table.astype(ml_dtypes.bfloat16)
    low = (table - high.astype(np.float64)).astype(ml_dtypes.bfloat16)
    return high, low


def rotation(outs, ins, sign):
    angles = sign * 2.0 * math.pi / LEN * ((outs[:, None] * ins[None, :]) % LEN)
    cosines = np.cos(angles) / math.sqrt(LEN)
    sines = np.sin(angles) / math.sqrt(LEN)
    return np.block([[cosines, -sines], [sines, cosines]])


@functools.lru_cache(None)
def tables(parts):
    grid = np.arange(LEN)
    thirds = np.arange(-HALF_THREE, HALF_THREE)
    row = np.arange(FIRSTS)
    firsts = PARTS * (row % STEP) + row // STEP - EDGE
    planes = LEN // parts
    order = np.arange(2 * LEN).reshape(2, parts, planes).transpose(1, 0, 2).ravel()
    beside = lambda table, axis: np.concatenate(split(table), axis=axis)
    return dict(
        three_in=beside(rotation(grid, thirds, 1)[order], 0),
        three_out=beside(rotation(thirds, grid, -1)[:, order], 0),
        two_in=beside(rotation(grid, grid, 1).T, 1),
        two_out=beside(rotation(grid, grid, -1).T, 1),
        one_in=beside(rotation(grid, firsts, 1), 0),
        one_out=beside(rotation(firsts, grid, -1), 0),
    )


def dot(a, b):
    return jnp.dot(a, b, preferred_element_type=F32)


def dot_nt(a, b):
    return lax.dot_general(a, b, NT, preferred_element_type=F32)


def halves(x):
    high = x.astype(BF16)
    return high, (x - high.astype(F32)).astype(BF16)


def fold(x, axis):
    half = x.shape[axis] // 2
    return x[:half] + x[half:] if axis == 0 else x[:, :half] + x[:, half:]


def one_hot(index, size):
    shape = (size, index.shape[1])
    return lax.broadcasted_iota(jnp.int32, shape, 0) == index


def third_slot(slot):
    return ((slot & (LEN - 1)) + HALF_THREE) & (LEN - 1)


def whole(*shape):
    return pl.BlockSpec(shape, lambda *_: (0,) * len(shape))


def spread_kernel(slot_ref, cols_ref, panel_ref, table_ref, out_ref, coef_ref, acc_ref):
    step = pl.program_id(0)
    cols = cols_ref.shape[1]
    count = panel_ref.shape[0]
    spans = [slice(at, at + LEN) for at in range(0, cols, LEN)]

    @pl.when(step == 0)
    def _():
        acc_ref[...] = jnp.zeros_like(acc_ref)

    slot = slot_ref[...]
    pick = one_hot(slot >> 7, cols).astype(BF16)
    panel = jnp.concatenate([panel_ref[:, part, :] for part in range(2)], axis=0)
    high = panel.astype(BF16)
    coef_ref[...] = high
    wide = high.astype(F32)
    values = jnp.concatenate([wide, panel - wide], axis=0).astype(BF16)
    third = jnp.broadcast_to(third_slot(slot).astype(F32), values.shape).astype(BF16)
    zero = jnp.zeros_like(values)
    rows = jnp.concatenate(
        [jnp.where(third == jnp.asarray(index, BF16), values, zero) for index in range(THIRDS)], axis=0
    )
    found = dot_nt(rows, pick)
    for at, span in enumerate(spans):
        acc_ref[at] += found[:, span]

    @pl.when(step == pl.num_programs(0) - 1)
    def _():
        owners = out_ref.shape[0]
        tall = table_ref.shape[0] // 2 // owners
        line = lambda row: jnp.concatenate(
            [acc_ref[at, pl.ds(row, THIRDS, stride=4 * count), :] for at in range(len(spans))], axis=1
        )
        for band in range(count):
            high = jnp.concatenate([line(band), line(count + band)], axis=0).astype(BF16)
            low = jnp.concatenate([line(2 * count + band), line(3 * count + band)], axis=0).astype(BF16)
            waves = fold(dot(table_ref[...], high), 0) + dot(table_ref[: owners * tall], low)
            out_ref[:, band * tall : (band + 1) * tall, :] = waves.astype(BF16).reshape(
                owners, tall, cols
            )
        column = cols_ref[...]
        place = lax.broadcasted_iota(jnp.int32, (8, cols), 0)
        names = jnp.where(place == 0, column >> 7, jnp.where(place == 1, column & (LEN - 1), 0))
        names = names.astype(F32).astype(BF16)
        for owner in range(owners):
            out_ref[owner, count * tall :, :] = names


def spread(panel, slot, columns, parts, chunk):
    count, _, waves = panel.shape
    cols = columns.shape[1]
    table = tables(parts)["three_in"]
    tall = 2 * LEN // parts
    return pl.pallas_call(
        spread_kernel,
        grid=(waves // chunk,),
        in_specs=[
            pl.BlockSpec((1, chunk), lambda i: (0, i)),
            whole(1, cols),
            pl.BlockSpec((count, 2, chunk), lambda i: (0, 0, i)),
            whole(*table.shape),
        ],
        out_specs=[
            whole(parts, count * tall + 8, cols),
            pl.BlockSpec((2 * count, chunk), lambda i: (0, i)),
        ],
        out_shape=[
            jax.ShapeDtypeStruct((parts, count * tall + 8, cols), BF16),
            jax.ShapeDtypeStruct((2 * count, waves), BF16),
        ],
        scratch_shapes=[pltpu.VMEM((cols // LEN, 4 * count * THIRDS, LEN), F32)],
        compiler_params=pltpu.CompilerParams(vmem_limit_bytes=56 << 20),
        cost_estimate=pl.CostEstimate(
            flops=2 * 4 * count * THIRDS * cols * waves, bytes_accessed=4 << 20, transcendentals=0
        ),
        name="spread",
    )(slot, columns, panel, jnp.asarray(table))


def grid_kernel(in_ref, pot_ref, ti_ref, oi_ref, oo_ref, to_ref, out_ref, pick_ref, first_ref, lhs_ref, found_ref, field_ref):
    owners, rows, cols = out_ref.shape
    planes = pot_ref.shape[0]
    tall = 2 * planes
    count = rows // tall

    for owner in range(owners):
        here = slice(owner * cols, (owner + 1) * cols)
        values = in_ref[owner].astype(F32)
        first = (values[rows : rows + 1].astype(jnp.int32) + EDGE) & (LEN - 1)
        inner = (first & (PARTS - 1)) * LEN + values[rows + 1 : rows + 2].astype(jnp.int32)
        pick_ref[:, here] = one_hot(inner, PARTS * LEN).astype(BF16)
        mask = one_hot(first // PARTS, STEP).astype(F32)
        first_ref[owner : owner + 1, :] = first // PARTS
        lhs_ref[:, here] = jnp.concatenate(
            [values[row : row + 1] * mask for row in range(rows)], axis=0
        ).astype(BF16)
    field = dot_nt(lhs_ref[...], pick_ref[...]).astype(BF16)
    block = planes * STEP
    lanes = lambda bit: slice(bit * LEN, (bit + 1) * LEN)
    spun = []
    for bit in range(PARTS):
        pair = jnp.concatenate(
            [
                jnp.concatenate(
                    [field[(2 * band + part) * block : (2 * band + part + 1) * block, lanes(bit)] for part in range(2)],
                    axis=1,
                )
                for band in range(count)
            ],
            axis=0,
        )
        spun.append(fold(dot(pair, ti_ref[...]), 1))
    tower = jnp.concatenate(
        [
            jnp.concatenate(
                [
                    spun[bit][item * STEP : (item + 1) * STEP, lanes(part)]
                    for part in range(2)
                    for bit in range(PARTS)
                ],
                axis=0,
            )
            for item in range(count * planes)
        ],
        axis=1,
    ).astype(BF16)
    psi = fold(dot(oi_ref[...], tower), 0)
    pot = jnp.concatenate([pot_ref[plane] for plane in range(planes)] * count, axis=1)
    psi = jnp.concatenate([psi[:LEN] * pot, psi[LEN:] * pot], axis=0).astype(BF16)
    back = fold(dot(oo_ref[...], psi), 0)
    bent = []
    for bit in range(PARTS):
        pair = jnp.concatenate(
            [
                jnp.concatenate(
                    [
                        back[
                            part * FIRSTS + bit * STEP : part * FIRSTS + (bit + 1) * STEP,
                            item * LEN : (item + 1) * LEN,
                        ]
                        for part in range(2)
                    ],
                    axis=1,
                )
                for item in range(count * planes)
            ],
            axis=0,
        ).astype(BF16)
        bent.append(fold(dot(pair, to_ref[...]), 1))
    for bit in range(PARTS):
        for item in range(count * planes):
            band, plane = divmod(item, planes)
            for part in range(2):
                found_ref[bit, pl.ds((2 * band + part) * planes + plane, USED, stride=rows), :] = bent[bit][
                    item * STEP : item * STEP + USED, lanes(part)
                ]
    for bit in range(PARTS):
        field_ref[:, lanes(bit)] = found_ref[bit].astype(BF16)
    for owner in range(owners):
        here = slice(owner * cols, (owner + 1) * cols)
        values = dot(field_ref[...], pick_ref[:, here])
        first = jnp.broadcast_to(first_ref[owner : owner + 1, :], (rows, cols))
        zero = jnp.zeros((rows, cols), F32)
        total = zero
        for at in range(USED):
            total += jnp.where(first == at, values[at * rows : (at + 1) * rows], zero)
        out_ref[owner] = total.astype(BF16)


def on_grid(waves, potential):
    owners, rows, cols = waves.shape
    rows -= 8
    pieces = [jnp.asarray(tables(owners)[name]) for name in ("two_in", "one_in", "one_out", "two_out")]
    return pl.pallas_call(
        grid_kernel,
        in_specs=[whole(*waves.shape), whole(*potential.shape)] + [whole(*piece.shape) for piece in pieces],
        out_specs=whole(owners, rows, cols),
        out_shape=jax.ShapeDtypeStruct((owners, rows, cols), BF16),
        scratch_shapes=[
            pltpu.VMEM((PARTS * LEN, owners * cols), BF16),
            pltpu.VMEM((owners, cols), jnp.int32),
            pltpu.VMEM((rows * STEP, owners * cols), BF16),
            pltpu.VMEM((PARTS, rows * USED, LEN), F32),
            pltpu.VMEM((rows * USED, PARTS * LEN), BF16),
        ],
        compiler_params=pltpu.CompilerParams(vmem_limit_bytes=56 << 20),
        cost_estimate=pl.CostEstimate(
            flops=2 * 2 * rows * USED * PARTS * LEN * owners * cols,
            bytes_accessed=4 << 20,
            transcendentals=0,
        ),
        name="on_grid",
    )(waves, potential, *pieces)


def collect_kernel(slot_ref, cols_ref, panel_ref, in_ref, table_ref, out_ref, wide_ref, held_ref):
    owners, rows, cols = in_ref.shape
    count = panel_ref.shape[0]
    tall = rows // count
    base = 2 * count * THIRDS

    @pl.when(pl.program_id(0) == 0)
    def _():
        for band in range(count):
            waves = in_ref[:, band * tall : (band + 1) * tall, :].reshape(owners * tall, cols)
            found = fold(dot(table_ref[...], waves), 0)
            for part in range(2):
                for at in range(cols // LEN):
                    wide_ref[at, pl.ds(part * count + band, THIRDS, stride=2 * count), :] = found[
                        part * THIRDS : (part + 1) * THIRDS, at * LEN : (at + 1) * LEN
                    ]
        for at in range(cols // LEN):
            high, low = halves(wide_ref[at])
            held_ref[:base, at * LEN : (at + 1) * LEN] = high
            held_ref[:base, cols + at * LEN : cols + (at + 1) * LEN] = low
        column = cols_ref[...]
        first = column >> 7
        second = column & (LEN - 1)
        first = jnp.where(first < LEN // 2, first, first - LEN)
        second = jnp.where(second < LEN // 2, second, second - LEN)
        size = first * first + second * second
        line = lax.broadcasted_iota(jnp.int32, (16, cols), 0)
        size = jnp.where(line == 0, size >> 7, jnp.where(line == 1, size & (LEN - 1), 0))
        held_ref[base:, :cols] = size.astype(F32).astype(BF16)
        held_ref[base:, cols:] = jnp.zeros((16, cols), BF16)

    slot = slot_ref[...]
    pick = one_hot(slot >> 7, cols).astype(BF16)
    third = third_slot(slot)
    found = dot(held_ref[...], jnp.concatenate([pick, pick], axis=0))
    panel = jnp.concatenate([panel_ref[:, part, :] for part in range(2)], axis=0)
    where = jnp.broadcast_to(third, panel.shape)
    zero = jnp.zeros_like(panel)
    tall = 2 * count
    back = [zero] * 4
    for index in range(THIRDS):
        back[index % 4] += jnp.where(where == index, found[index * tall : (index + 1) * tall], zero)
    third = (third - HALF_THREE).astype(F32)
    kinetic = (float(LEN) * found[base : base + 1] + found[base + 1 : base + 2] + third * third) * (
        2.0 / LEN**2
    )
    out_ref[...] = (kinetic * panel + ((back[0] + back[1]) + (back[2] + back[3]))).astype(BF16)


def collect(panel, slot, columns, waves, start, length, chunk):
    count = panel.shape[0]
    owners, rows, cols = waves.shape
    table = tables(owners)["three_out"]
    skip = start // chunk
    return pl.pallas_call(
        collect_kernel,
        grid=(length // chunk,),
        in_specs=[
            pl.BlockSpec((1, chunk), lambda i: (0, i + skip)),
            whole(1, cols),
            pl.BlockSpec((count, 2, chunk), lambda i: (0, 0, i + skip)),
            whole(*waves.shape),
            whole(*table.shape),
        ],
        out_specs=pl.BlockSpec((2 * count, chunk), lambda i: (0, i)),
        out_shape=jax.ShapeDtypeStruct((2 * count, length), BF16),
        scratch_shapes=[
            pltpu.VMEM((cols // LEN, 2 * count * THIRDS, LEN), F32),
            pltpu.VMEM((2 * count * THIRDS + 16, 2 * cols), BF16),
        ],
        compiler_params=pltpu.CompilerParams(vmem_limit_bytes=40 << 20),
        cost_estimate=pl.CostEstimate(
            flops=2 * 4 * count * THIRDS * cols * length, bytes_accessed=4 << 20, transcendentals=0
        ),
        name="collect",
    )(slot, columns, panel, waves, jnp.asarray(table))


def project_kernel(sizes, seat_ref, *refs):
    pieces, (both_ref, prev_ref, out_ref, acc_ref) = refs[: len(sizes)], refs[len(sizes) :]
    step = pl.program_id(0)

    @pl.when(step == 0)
    def _():
        acc_ref[...] = jnp.zeros_like(acc_ref)

    rows = jnp.concatenate([ref[...].reshape(-1, ref.shape[-1]) for ref in pieces], axis=0)
    acc_ref[...] += dot_nt(rows, both_ref[...])

    @pl.when(step == pl.num_programs(0) - 1)
    def _():
        half = acc_ref.shape[1] // 2
        out_ref[...] = prev_ref[...]
        blocks = []
        for piece in range(acc_ref.shape[0] // 8):
            real = acc_ref[8 * piece : 8 * piece + 4]
            imag = acc_ref[8 * piece + 4 : 8 * piece + 8]
            blocks.append((real[:, :half] + imag[:, half:], imag[:, :half] - real[:, half:]))
        for pair in range(len(blocks) // 2):
            odd = seat_ref[8] == 1
            for part in range(2):
                one, two = blocks[2 * pair][part], blocks[2 * pair + 1][part]
                tile = jnp.concatenate([jnp.where(odd, two, one), jnp.where(odd, one, two)], axis=0)
                seat = seat_ref[pair] + part * (len(blocks) // 2)
                out_ref[seat] = out_ref[seat] + tile


def project(pieces, both, prev, seats, start, chunk):
    length = pieces[0].shape[-1]
    sizes = [math.prod(piece.shape[:-1]) for piece in pieces]
    skip = start // chunk
    block = lambda piece: pl.BlockSpec(
        piece.shape[:-1] + (chunk,), lambda i, *_, n=piece.ndim: (0,) * (n - 1) + (i,)
    )
    return pl.pallas_call(
        functools.partial(project_kernel, sizes),
        grid_spec=pltpu.PrefetchScalarGridSpec(
            num_scalar_prefetch=1,
            grid=(length // chunk,),
            in_specs=[block(piece) for piece in pieces]
            + [
                pl.BlockSpec((both.shape[0], chunk), lambda i, *_: (0, i + skip)),
                whole(*prev.shape),
            ],
            out_specs=whole(*prev.shape),
            scratch_shapes=[pltpu.VMEM((sum(sizes), both.shape[0]), F32)],
        ),
        out_shape=jax.ShapeDtypeStruct(prev.shape, F32),
        compiler_params=pltpu.CompilerParams(vmem_limit_bytes=32 << 20),
        cost_estimate=pl.CostEstimate(
            flops=2 * 256 * both.shape[0] * length,
            bytes_accessed=2 * both.shape[0] * length,
            transcendentals=0,
        ),
        name="project",
    )(seats, *pieces, both, prev)


def moved(x, axis, target):
    size = lax.axis_size(axis)
    return lax.ppermute(x, axis, [(i, target(i) % size) for i in range(size)])


def share(x, meanwhile):
    pair = jnp.stack([x, moved(x, "band", lambda i: i ^ 1)])
    pair, meanwhile = lax.optimization_barrier((pair, meanwhile))
    below = moved(pair, "band", lambda i: i + 2)
    above = moved(pair, "band", lambda i: i - 2)
    far = [moved(below[0], "band", lambda i: i + 2), moved(above[1], "band", lambda i: i - 2)]
    return [pair, below, above] + far, meanwhile


def per_device(slab, panel, potential, pw_slot, columns):
    parts = lax.axis_size("pw")
    bands, _, length = slab.shape
    cols = columns.shape[0]
    slot = pw_slot.reshape(1, length)
    columns = columns.reshape(1, cols)
    waves, coeffs = spread(panel, slot, columns, parts, 3072)
    waves = lax.all_to_all(waves, "pw", split_axis=0, concat_axis=0, tiled=True)
    coeffs = lax.all_gather(coeffs, "band", axis=0, tiled=True)
    both = jnp.transpose(slab, (1, 0, 2)).reshape(2 * bands, length)
    waves, both = lax.optimization_barrier((waves, both))
    waves = on_grid(waves, potential)
    waves = lax.all_to_all(waves, "pw", split_axis=0, concat_axis=0, tiled=True)
    waves, coeffs = lax.optimization_barrier((waves, coeffs))
    me = lax.axis_index("band")
    row, odd = me // 2, me % 2
    terms = jnp.zeros((parts, bands // parts, bands), F32)
    pick = lambda *seats: jnp.stack([jnp.asarray(seat, jnp.int32) for seat in seats])
    applied = collect(panel, slot, columns, waves, 0, length, 3072)
    seats = pick(8, 9, 10, 11, 0, 0, 0, 0, 0)
    terms = project([coeffs], both, terms, seats, 0, 3072)
    shared, terms = share(applied, terms)
    seats = pick(row, (row + 3) % 4, (row + 1) % 4, (row + 2) % 4, 0, 0, 0, 0, odd)
    terms = project(shared, both, terms, seats, 0, 3072)
    terms = lax.all_to_all(terms, "pw", split_axis=0, concat_axis=0, tiled=True)
    return jnp.sum(terms, axis=0).T


def solution(mesh):
    in_specs = (P("band", None, "pw"), P("band", None, "pw"), P("pw", None, None), P("pw"), P("pw"))
    out_specs = P("band", "pw")
    return jax.shard_map(
        per_device, mesh=mesh, in_specs=in_specs, out_specs=out_specs, check_vma=False
    )
```

```python
import functools
import math

import jax
import jax.numpy as jnp
import ml_dtypes
import numpy as np
from jax import lax
from jax.experimental import pallas as pl
from jax.experimental.pallas import tpu as pltpu
from jax.sharding import PartitionSpec as P

F32 = jnp.float32
BF16 = jnp.bfloat16
LEN = 128
HALF_THREE = 44
THIRDS = 2 * HALF_THREE
EDGE = 40
PARTS = 4
STEP = 24
USED = 20
FIRSTS = PARTS * STEP
NT = (((1,), (1,)), ((), ()))


def split(table):
    high = table.astype(ml_dtypes.bfloat16)
    low = (table - high.astype(np.float64)).astype(ml_dtypes.bfloat16)
    return high, low


def rotation(outs, ins, sign):
    angles = sign * 2.0 * math.pi / LEN * ((outs[:, None] * ins[None, :]) % LEN)
    cosines = np.cos(angles) / math.sqrt(LEN)
    sines = np.sin(angles) / math.sqrt(LEN)
    return np.block([[cosines, -sines], [sines, cosines]])


@functools.lru_cache(None)
def tables(parts):
    grid = np.arange(LEN)
    thirds = np.arange(-HALF_THREE, HALF_THREE)
    row = np.arange(FIRSTS)
    firsts = PARTS * (row % STEP) + row // STEP - EDGE
    planes = LEN // parts
    order = np.arange(2 * LEN).reshape(2, parts, planes).transpose(1, 0, 2).ravel()
    beside = lambda table, axis: np.concatenate(split(table), axis=axis)
    return dict(
        three_in=beside(rotation(grid, thirds, 1)[order], 0),
        three_out=beside(rotation(thirds, grid, -1)[:, order], 0),
        two_in=beside(rotation(grid, grid, 1).T, 1),
        two_out=beside(rotation(grid, grid, -1).T, 1),
        one_in=beside(rotation(grid, firsts, 1), 0),
        one_out=beside(rotation(firsts, grid, -1), 0),
    )


def dot(a, b):
    return jnp.dot(a, b, preferred_element_type=F32)


def dot_nt(a, b):
    return lax.dot_general(a, b, NT, preferred_element_type=F32)


def halves(x):
    high = x.astype(BF16)
    return high, (x - high.astype(F32)).astype(BF16)


def fold(x, axis):
    half = x.shape[axis] // 2
    return x[:half] + x[half:] if axis == 0 else x[:, :half] + x[:, half:]


def one_hot(index, size):
    shape = (size, index.shape[1])
    return lax.broadcasted_iota(jnp.int32, shape, 0) == index


def third_slot(slot):
    return ((slot & (LEN - 1)) + HALF_THREE) & (LEN - 1)


def whole(*shape):
    return pl.BlockSpec(shape, lambda *_: (0,) * len(shape))


def spread_kernel(slot_ref, cols_ref, panel_ref, table_ref, out_ref, coef_ref, acc_ref):
    step = pl.program_id(0)
    cols = cols_ref.shape[1]
    count = panel_ref.shape[0]
    spans = [slice(at, at + LEN) for at in range(0, cols, LEN)]

    @pl.when(step == 0)
    def _():
        acc_ref[...] = jnp.zeros_like(acc_ref)

    slot = slot_ref[...]
    pick = one_hot(slot >> 7, cols).astype(BF16)
    panel = jnp.concatenate([panel_ref[:, part, :] for part in range(2)], axis=0)
    high = panel.astype(BF16)
    coef_ref[...] = high
    wide = high.astype(F32)
    values = jnp.concatenate([wide, panel - wide], axis=0).astype(BF16)
    third = jnp.broadcast_to(third_slot(slot).astype(F32), values.shape).astype(BF16)
    zero = jnp.zeros_like(values)
    rows = jnp.concatenate(
        [jnp.where(third == jnp.asarray(index, BF16), values, zero) for index in range(THIRDS)], axis=0
    )
    found = dot_nt(rows, pick)
    for at, span in enumerate(spans):
        acc_ref[at] += found[:, span]

    @pl.when(step == pl.num_programs(0) - 1)
    def _():
        owners = out_ref.shape[0]
        tall = table_ref.shape[0] // 2 // owners
        line = lambda row: jnp.concatenate(
            [acc_ref[at, pl.ds(row, THIRDS, stride=4 * count), :] for at in range(len(spans))], axis=1
        )
        for band in range(count):
            high = jnp.concatenate([line(band), line(count + band)], axis=0).astype(BF16)
            low = jnp.concatenate([line(2 * count + band), line(3 * count + band)], axis=0).astype(BF16)
            waves = fold(dot(table_ref[...], high), 0) + dot(table_ref[: owners * tall], low)
            out_ref[:, band * tall : (band + 1) * tall, :] = waves.astype(BF16).reshape(
                owners, tall, cols
            )
        column = cols_ref[...]
        place = lax.broadcasted_iota(jnp.int32, (8, cols), 0)
        names = jnp.where(place == 0, column >> 7, jnp.where(place == 1, column & (LEN - 1), 0))
        names = names.astype(F32).astype(BF16)
        for owner in range(owners):
            out_ref[owner, count * tall :, :] = names


def spread(panel, slot, columns, parts, chunk):
    count, _, waves = panel.shape
    cols = columns.shape[1]
    table = tables(parts)["three_in"]
    tall = 2 * LEN // parts
    return pl.pallas_call(
        spread_kernel,
        grid=(waves // chunk,),
        in_specs=[
            pl.BlockSpec((1, chunk), lambda i: (0, i)),
            whole(1, cols),
            pl.BlockSpec((count, 2, chunk), lambda i: (0, 0, i)),
            whole(*table.shape),
        ],
        out_specs=[
            whole(parts, count * tall + 8, cols),
            pl.BlockSpec((2 * count, chunk), lambda i: (0, i)),
        ],
        out_shape=[
            jax.ShapeDtypeStruct((parts, count * tall + 8, cols), BF16),
            jax.ShapeDtypeStruct((2 * count, waves), BF16),
        ],
        scratch_shapes=[pltpu.VMEM((cols // LEN, 4 * count * THIRDS, LEN), F32)],
        compiler_params=pltpu.CompilerParams(vmem_limit_bytes=56 << 20),
        cost_estimate=pl.CostEstimate(
            flops=2 * 4 * count * THIRDS * cols * waves, bytes_accessed=4 << 20, transcendentals=0
        ),
        name="spread",
    )(slot, columns, panel, jnp.asarray(table))


def grid_kernel(in_ref, pot_ref, ti_ref, oi_ref, oo_ref, to_ref, out_ref, pick_ref, first_ref, lhs_ref, found_ref, field_ref):
    owners, rows, cols = out_ref.shape
    planes = pot_ref.shape[0]
    tall = 2 * planes
    count = rows // tall

    for owner in range(owners):
        here = slice(owner * cols, (owner + 1) * cols)
        values = in_ref[owner].astype(F32)
        first = (values[rows : rows + 1].astype(jnp.int32) + EDGE) & (LEN - 1)
        inner = (first & (PARTS - 1)) * LEN + values[rows + 1 : rows + 2].astype(jnp.int32)
        pick_ref[:, here] = one_hot(inner, PARTS * LEN).astype(BF16)
        mask = one_hot(first // PARTS, STEP).astype(F32)
        first_ref[owner : owner + 1, :] = first // PARTS
        lhs_ref[:, here] = jnp.concatenate(
            [values[row : row + 1] * mask for row in range(rows)], axis=0
        ).astype(BF16)
    field = dot_nt(lhs_ref[...], pick_ref[...]).astype(BF16)
    block = planes * STEP
    lanes = lambda bit: slice(bit * LEN, (bit + 1) * LEN)
    spun = []
    for bit in range(PARTS):
        pair = jnp.concatenate(
            [
                jnp.concatenate(
                    [field[(2 * band + part) * block : (2 * band + part + 1) * block, lanes(bit)] for part in range(2)],
                    axis=1,
                )
                for band in range(count)
            ],
            axis=0,
        )
        spun.append(fold(dot(pair, ti_ref[...]), 1))
    tower = jnp.concatenate(
        [
            jnp.concatenate(
                [
                    spun[bit][item * STEP : (item + 1) * STEP, lanes(part)]
                    for part in range(2)
                    for bit in range(PARTS)
                ],
                axis=0,
            )
            for item in range(count * planes)
        ],
        axis=1,
    ).astype(BF16)
    psi = fold(dot(oi_ref[...], tower), 0)
    pot = jnp.concatenate([pot_ref[plane] for plane in range(planes)] * count, axis=1)
    psi = jnp.concatenate([psi[:LEN] * pot, psi[LEN:] * pot], axis=0).astype(BF16)
    back = fold(dot(oo_ref[...], psi), 0)
    bent = []
    for bit in range(PARTS):
        pair = jnp.concatenate(
            [
                jnp.concatenate(
                    [
                        back[
                            part * FIRSTS + bit * STEP : part * FIRSTS + (bit + 1) * STEP,
                            item * LEN : (item + 1) * LEN,
                        ]
                        for part in range(2)
                    ],
                    axis=1,
                )
                for item in range(count * planes)
            ],
            axis=0,
        ).astype(BF16)
        bent.append(fold(dot(pair, to_ref[...]), 1))
    for bit in range(PARTS):
        for item in range(count * planes):
            band, plane = divmod(item, planes)
            for part in range(2):
                found_ref[bit, pl.ds((2 * band + part) * planes + plane, USED, stride=rows), :] = bent[bit][
                    item * STEP : item * STEP + USED, lanes(part)
                ]
    for bit in range(PARTS):
        field_ref[:, lanes(bit)] = found_ref[bit].astype(BF16)
    for owner in range(owners):
        here = slice(owner * cols, (owner + 1) * cols)
        values = dot(field_ref[...], pick_ref[:, here])
        first = jnp.broadcast_to(first_ref[owner : owner + 1, :], (rows, cols))
        zero = jnp.zeros((rows, cols), F32)
        total = zero
        for at in range(USED):
            total += jnp.where(first == at, values[at * rows : (at + 1) * rows], zero)
        out_ref[owner] = total.astype(BF16)


def on_grid(waves, potential):
    owners, rows, cols = waves.shape
    rows -= 8
    pieces = [jnp.asarray(tables(owners)[name]) for name in ("two_in", "one_in", "one_out", "two_out")]
    return pl.pallas_call(
        grid_kernel,
        in_specs=[whole(*waves.shape), whole(*potential.shape)] + [whole(*piece.shape) for piece in pieces],
        out_specs=whole(owners, rows, cols),
        out_shape=jax.ShapeDtypeStruct((owners, rows, cols), BF16),
        scratch_shapes=[
            pltpu.VMEM((PARTS * LEN, owners * cols), BF16),
            pltpu.VMEM((owners, cols), jnp.int32),
            pltpu.VMEM((rows * STEP, owners * cols), BF16),
            pltpu.VMEM((PARTS, rows * USED, LEN), F32),
            pltpu.VMEM((rows * USED, PARTS * LEN), BF16),
        ],
        compiler_params=pltpu.CompilerParams(vmem_limit_bytes=56 << 20),
        cost_estimate=pl.CostEstimate(
            flops=2 * 2 * rows * USED * PARTS * LEN * owners * cols,
            bytes_accessed=4 << 20,
            transcendentals=0,
        ),
        name="on_grid",
    )(waves, potential, *pieces)


def collect_kernel(slot_ref, cols_ref, panel_ref, in_ref, table_ref, out_ref, wide_ref, held_ref):
    owners, rows, cols = in_ref.shape
    count = panel_ref.shape[0]
    tall = rows // count
    base = 2 * count * THIRDS

    @pl.when(pl.program_id(0) == 0)
    def _():
        for band in range(count):
            waves = in_ref[:, band * tall : (band + 1) * tall, :].reshape(owners * tall, cols)
            found = fold(dot(table_ref[...], waves), 0)
            for part in range(2):
                for at in range(cols // LEN):
                    wide_ref[at, pl.ds(part * count + band, THIRDS, stride=2 * count), :] = found[
                        part * THIRDS : (part + 1) * THIRDS, at * LEN : (at + 1) * LEN
                    ]
        for at in range(cols // LEN):
            high, low = halves(wide_ref[at])
            held_ref[:base, at * LEN : (at + 1) * LEN] = high
            held_ref[:base, cols + at * LEN : cols + (at + 1) * LEN] = low
        column = cols_ref[...]
        first = column >> 7
        second = column & (LEN - 1)
        first = jnp.where(first < LEN // 2, first, first - LEN)
        second = jnp.where(second < LEN // 2, second, second - LEN)
        size = first * first + second * second
        line = lax.broadcasted_iota(jnp.int32, (16, cols), 0)
        size = jnp.where(line == 0, size >> 7, jnp.where(line == 1, size & (LEN - 1), 0))
        held_ref[base:, :cols] = size.astype(F32).astype(BF16)
        held_ref[base:, cols:] = jnp.zeros((16, cols), BF16)

    slot = slot_ref[...]
    pick = one_hot(slot >> 7, cols).astype(BF16)
    third = third_slot(slot)
    found = dot(held_ref[...], jnp.concatenate([pick, pick], axis=0))
    panel = jnp.concatenate([panel_ref[:, part, :] for part in range(2)], axis=0)
    where = jnp.broadcast_to(third, panel.shape)
    zero = jnp.zeros_like(panel)
    tall = 2 * count
    back = [zero] * 4
    for index in range(THIRDS):
        back[index % 4] += jnp.where(where == index, found[index * tall : (index + 1) * tall], zero)
    third = (third - HALF_THREE).astype(F32)
    kinetic = (float(LEN) * found[base : base + 1] + found[base + 1 : base + 2] + third * third) * (
        2.0 / LEN**2
    )
    out_ref[...] = (kinetic * panel + ((back[0] + back[1]) + (back[2] + back[3]))).astype(BF16)


def collect(panel, slot, columns, waves, start, length, chunk):
    count = panel.shape[0]
    owners, rows, cols = waves.shape
    table = tables(owners)["three_out"]
    skip = start // chunk
    return pl.pallas_call(
        collect_kernel,
        grid=(length // chunk,),
        in_specs=[
            pl.BlockSpec((1, chunk), lambda i: (0, i + skip)),
            whole(1, cols),
            pl.BlockSpec((count, 2, chunk), lambda i: (0, 0, i + skip)),
            whole(*waves.shape),
            whole(*table.shape),
        ],
        out_specs=pl.BlockSpec((2 * count, chunk), lambda i: (0, i)),
        out_shape=jax.ShapeDtypeStruct((2 * count, length), BF16),
        scratch_shapes=[
            pltpu.VMEM((cols // LEN, 2 * count * THIRDS, LEN), F32),
            pltpu.VMEM((2 * count * THIRDS + 16, 2 * cols), BF16),
        ],
        compiler_params=pltpu.CompilerParams(vmem_limit_bytes=40 << 20),
        cost_estimate=pl.CostEstimate(
            flops=2 * 4 * count * THIRDS * cols * length, bytes_accessed=4 << 20, transcendentals=0
        ),
        name="collect",
    )(slot, columns, panel, waves, jnp.asarray(table))


def project_kernel(sizes, seat_ref, *refs):
    pieces, (both_ref, prev_ref, out_ref, acc_ref) = refs[: len(sizes)], refs[len(sizes) :]
    step = pl.program_id(0)

    @pl.when(step == 0)
    def _():
        acc_ref[...] = jnp.zeros_like(acc_ref)

    chunk = both_ref.shape[1]
    here = pl.ds(pl.multiple_of(step * chunk, chunk), chunk)
    rows = jnp.concatenate([ref[:, here] for ref in pieces], axis=0)
    acc_ref[...] += dot_nt(rows, both_ref[...])

    @pl.when(step == pl.num_programs(0) - 1)
    def _():
        half = acc_ref.shape[1] // 2
        out_ref[...] = prev_ref[...]
        blocks = []
        for piece in range(acc_ref.shape[0] // 8):
            real = acc_ref[8 * piece : 8 * piece + 4]
            imag = acc_ref[8 * piece + 4 : 8 * piece + 8]
            blocks.append((real[:, :half] + imag[:, half:], imag[:, :half] - real[:, half:]))
        for pair in range(len(blocks) // 2):
            odd = seat_ref[8] == 1
            for part in range(2):
                one, two = blocks[2 * pair][part], blocks[2 * pair + 1][part]
                tile = jnp.concatenate([jnp.where(odd, two, one), jnp.where(odd, one, two)], axis=0)
                seat = seat_ref[pair] + part * (len(blocks) // 2)
                out_ref[seat] = out_ref[seat] + tile


def project(pieces, both, prev, seats, start, chunk):
    length = pieces[0].shape[-1]
    sizes = [math.prod(piece.shape[:-1]) for piece in pieces]
    skip = start // chunk
    return pl.pallas_call(
        functools.partial(project_kernel, sizes),
        grid_spec=pltpu.PrefetchScalarGridSpec(
            num_scalar_prefetch=1,
            grid=(length // chunk,),
            in_specs=[whole(*piece.shape) for piece in pieces]
            + [
                pl.BlockSpec((both.shape[0], chunk), lambda i, *_: (0, i + skip)),
                whole(*prev.shape),
            ],
            out_specs=whole(*prev.shape),
            scratch_shapes=[pltpu.VMEM((sum(sizes), both.shape[0]), F32)],
        ),
        out_shape=jax.ShapeDtypeStruct(prev.shape, F32),
        compiler_params=pltpu.CompilerParams(vmem_limit_bytes=56 << 20),
        cost_estimate=pl.CostEstimate(
            flops=2 * 256 * both.shape[0] * length,
            bytes_accessed=2 * both.shape[0] * length,
            transcendentals=0,
        ),
        name="project",
    )(seats, *pieces, both, prev)


def moved(x, axis, target):
    size = lax.axis_size(axis)
    return lax.ppermute(x, axis, [(i, target(i) % size) for i in range(size)])


def share(x, meanwhile):
    other = moved(x, "band", lambda i: i ^ 1)
    below = [moved(x, "band", lambda i: i + 2)]
    above = [moved(x, "band", lambda i: i - 2)]
    above.append(moved(other, "band", lambda i: i - 2))
    below.append(moved(other, "band", lambda i: i + 2))
    first, second, meanwhile = lax.optimization_barrier((below[0], above[1], meanwhile))
    far = [moved(first, "band", lambda i: i + 2), moved(second, "band", lambda i: i - 2)]
    return [x, other] + below + above + far, meanwhile


def per_device(slab, panel, potential, pw_slot, columns):
    parts = lax.axis_size("pw")
    bands, _, length = slab.shape
    cols = columns.shape[0]
    slot = pw_slot.reshape(1, length)
    columns = columns.reshape(1, cols)
    waves, coeffs = spread(panel, slot, columns, parts, 3072)
    waves = lax.all_to_all(waves, "pw", split_axis=0, concat_axis=0, tiled=True)
    coeffs = lax.all_gather(coeffs, "band", axis=0, tiled=True)
    both = jnp.transpose(slab, (1, 0, 2)).reshape(2 * bands, length)
    waves, both = lax.optimization_barrier((waves, both))
    waves = on_grid(waves, potential)
    waves = lax.all_to_all(waves, "pw", split_axis=0, concat_axis=0, tiled=True)
    waves, coeffs = lax.optimization_barrier((waves, coeffs))
    me = lax.axis_index("band")
    row, odd = me // 2, me % 2
    terms = jnp.zeros((parts, bands // parts, bands), F32)
    pick = lambda *seats: jnp.stack([jnp.asarray(seat, jnp.int32) for seat in seats])
    applied = collect(panel, slot, columns, waves, 0, length, 3072)
    seats = pick(8, 9, 10, 11, 0, 0, 0, 0, 0)
    terms = project([coeffs], both, terms, seats, 0, 3072)
    shared, terms = share(applied, terms)
    seats = pick(row, (row + 3) % 4, (row + 1) % 4, (row + 2) % 4, 0, 0, 0, 0, odd)
    terms = project(shared, both, terms, seats, 0, 3072)
    terms = lax.all_to_all(terms, "pw", split_axis=0, concat_axis=0, tiled=True)
    return jnp.sum(terms, axis=0).T


def solution(mesh):
    in_specs = (P("band", None, "pw"), P("band", None, "pw"), P("pw", None, None), P("pw"), P("pw"))
    out_specs = P("band", "pw")
    return jax.shard_map(
        per_device, mesh=mesh, in_specs=in_specs, out_specs=out_specs, check_vma=False
    )
```

```python
import functools
import math

import jax
import jax.numpy as jnp
import ml_dtypes
import numpy as np
from jax import lax
from jax.experimental import pallas as pl
from jax.experimental.pallas import tpu as pltpu
from jax.sharding import PartitionSpec as P

F32 = jnp.float32
BF16 = jnp.bfloat16
LEN = 128
HALF_THREE = 44
THIRDS = 2 * HALF_THREE
EDGE = 40
PARTS = 4
STEP = 24
USED = 20
GROUP = 4
FIRSTS = PARTS * STEP
NT = (((1,), (1,)), ((), ()))


def split(table):
    high = table.astype(ml_dtypes.bfloat16)
    low = (table - high.astype(np.float64)).astype(ml_dtypes.bfloat16)
    return high, low


def rotation(outs, ins, sign):
    angles = sign * 2.0 * math.pi / LEN * ((outs[:, None] * ins[None, :]) % LEN)
    cosines = np.cos(angles) / math.sqrt(LEN)
    sines = np.sin(angles) / math.sqrt(LEN)
    return np.block([[cosines, -sines], [sines, cosines]])


@functools.lru_cache(None)
def tables(parts):
    grid = np.arange(LEN)
    thirds = np.arange(-HALF_THREE, HALF_THREE)
    row = np.arange(FIRSTS)
    firsts = PARTS * (row % STEP) + row // STEP - EDGE
    planes = LEN // parts
    order = np.arange(2 * LEN).reshape(2, parts, planes).transpose(1, 0, 2).ravel()
    beside = lambda table, axis: np.concatenate(split(table), axis=axis)
    return dict(
        three_in=beside(rotation(grid, thirds, 1)[order], 0),
        three_out=beside(rotation(thirds, grid, -1)[:, order], 0),
        two_in=beside(rotation(grid, grid, 1).T, 1),
        two_out=beside(rotation(grid, grid, -1).T, 1),
        one_in=beside(rotation(grid, firsts, 1), 0),
        one_out=beside(rotation(firsts, grid, -1), 0),
    )


def dot(a, b):
    return jnp.dot(a, b, preferred_element_type=F32)


def dot_nt(a, b):
    return lax.dot_general(a, b, NT, preferred_element_type=F32)


def halves(x):
    high = x.astype(BF16)
    return high, (x - high.astype(F32)).astype(BF16)


def fold(x, axis):
    half = x.shape[axis] // 2
    return x[:half] + x[half:] if axis == 0 else x[:, :half] + x[:, half:]


def one_hot(index, size):
    shape = (size, index.shape[1])
    return lax.broadcasted_iota(jnp.int32, shape, 0) == index


def third_slot(slot):
    return ((slot & (LEN - 1)) + HALF_THREE) & (LEN - 1)


def whole(*shape):
    return pl.BlockSpec(shape, lambda *_: (0,) * len(shape))


def spread_kernel(slot_ref, cols_ref, panel_ref, table_ref, out_ref, coef_ref, acc_ref):
    step = pl.program_id(0)
    cols = cols_ref.shape[1]
    count = panel_ref.shape[0]
    spans = [slice(at, at + LEN) for at in range(0, cols, LEN)]

    @pl.when(step == 0)
    def _():
        acc_ref[...] = jnp.zeros_like(acc_ref)

    slot = slot_ref[...]
    pick = one_hot(slot >> 7, cols).astype(BF16)
    panel = jnp.concatenate([panel_ref[:, part, :] for part in range(2)], axis=0)
    high = panel.astype(BF16)
    coef_ref[...] = high
    wide = high.astype(F32)
    values = jnp.concatenate([wide, panel - wide], axis=0).astype(BF16)
    third = jnp.broadcast_to(third_slot(slot).astype(F32), values.shape).astype(BF16)
    zero = jnp.zeros_like(values)
    rows = jnp.concatenate(
        [jnp.where(third == jnp.asarray(index, BF16), values, zero) for index in range(THIRDS)], axis=0
    )
    found = dot_nt(rows, pick)
    for at, span in enumerate(spans):
        acc_ref[at] += found[:, span]

    @pl.when(step == pl.num_programs(0) - 1)
    def _():
        owners = out_ref.shape[0]
        tall = table_ref.shape[0] // 2 // owners
        line = lambda row: jnp.concatenate(
            [acc_ref[at, pl.ds(row, THIRDS, stride=4 * count), :] for at in range(len(spans))], axis=1
        )
        for band in range(count):
            high = jnp.concatenate([line(band), line(count + band)], axis=0).astype(BF16)
            low = jnp.concatenate([line(2 * count + band), line(3 * count + band)], axis=0).astype(BF16)
            waves = fold(dot(table_ref[...], high), 0) + dot(table_ref[: owners * tall], low)
            out_ref[:, band * tall : (band + 1) * tall, :] = waves.astype(BF16).reshape(
                owners, tall, cols
            )
        column = cols_ref[...]
        place = lax.broadcasted_iota(jnp.int32, (8, cols), 0)
        names = jnp.where(place == 0, column >> 7, jnp.where(place == 1, column & (LEN - 1), 0))
        names = names.astype(F32).astype(BF16)
        for owner in range(owners):
            out_ref[owner, count * tall :, :] = names


def spread(panel, slot, columns, parts, chunk):
    count, _, waves = panel.shape
    cols = columns.shape[1]
    table = tables(parts)["three_in"]
    tall = 2 * LEN // parts
    return pl.pallas_call(
        spread_kernel,
        grid=(waves // chunk,),
        in_specs=[
            pl.BlockSpec((1, chunk), lambda i: (0, i)),
            whole(1, cols),
            pl.BlockSpec((count, 2, chunk), lambda i: (0, 0, i)),
            whole(*table.shape),
        ],
        out_specs=[
            whole(parts, count * tall + 8, cols),
            pl.BlockSpec((2 * count, chunk), lambda i: (0, i)),
        ],
        out_shape=[
            jax.ShapeDtypeStruct((parts, count * tall + 8, cols), BF16),
            jax.ShapeDtypeStruct((2 * count, waves), BF16),
        ],
        scratch_shapes=[pltpu.VMEM((cols // LEN, 4 * count * THIRDS, LEN), F32)],
        compiler_params=pltpu.CompilerParams(vmem_limit_bytes=56 << 20),
        cost_estimate=pl.CostEstimate(
            flops=2 * 4 * count * THIRDS * cols * waves, bytes_accessed=4 << 20, transcendentals=0
        ),
        name="spread",
    )(slot, columns, panel, jnp.asarray(table))


def grid_kernel(in_ref, pot_ref, ti_ref, oi_ref, oo_ref, to_ref, out_ref, pick_ref, first_ref, lhs_ref, found_ref, field_ref):
    owners, rows, cols = out_ref.shape
    planes = pot_ref.shape[0]
    tall = 2 * planes
    count = rows // tall

    field = None
    for owner in range(owners):
        here = slice(owner * cols, (owner + 1) * cols)
        values = in_ref[owner].astype(F32)
        first = (values[rows : rows + 1].astype(jnp.int32) + EDGE) & (LEN - 1)
        inner = (first & (PARTS - 1)) * LEN + values[rows + 1 : rows + 2].astype(jnp.int32)
        pick_ref[:, here] = one_hot(inner, PARTS * LEN).astype(BF16)
        mask = one_hot(first // PARTS, STEP).astype(F32)
        first_ref[owner : owner + 1, :] = first // PARTS
        lhs_ref[:, here] = jnp.concatenate(
            [values[row : row + 1] * mask for row in range(rows)], axis=0
        ).astype(BF16)
        if (owner + 1) % GROUP == 0:
            group = slice((owner + 1 - GROUP) * cols, (owner + 1) * cols)
            found = dot_nt(lhs_ref[:, group], pick_ref[:, group])
            field = found if field is None else field + found
    field = field.astype(BF16)
    block = planes * STEP
    lanes = lambda bit: slice(bit * LEN, (bit + 1) * LEN)
    spun = []
    for bit in range(PARTS):
        pair = jnp.concatenate(
            [
                jnp.concatenate(
                    [field[(2 * band + part) * block : (2 * band + part + 1) * block, lanes(bit)] for part in range(2)],
                    axis=1,
                )
                for band in range(count)
            ],
            axis=0,
        )
        spun.append(fold(dot(pair, ti_ref[...]), 1))
    tower = jnp.concatenate(
        [
            jnp.concatenate(
                [
                    spun[bit][item * STEP : (item + 1) * STEP, lanes(part)]
                    for part in range(2)
                    for bit in range(PARTS)
                ],
                axis=0,
            )
            for item in range(count * planes)
        ],
        axis=1,
    ).astype(BF16)
    psi = fold(dot(oi_ref[...], tower), 0)
    pot = jnp.concatenate([pot_ref[plane] for plane in range(planes)] * count, axis=1)
    psi = jnp.concatenate([psi[:LEN] * pot, psi[LEN:] * pot], axis=0).astype(BF16)
    back = fold(dot(oo_ref[...], psi), 0)
    bent = []
    for bit in range(PARTS):
        pair = jnp.concatenate(
            [
                jnp.concatenate(
                    [
                        back[
                            part * FIRSTS + bit * STEP : part * FIRSTS + (bit + 1) * STEP,
                            item * LEN : (item + 1) * LEN,
                        ]
                        for part in range(2)
                    ],
                    axis=1,
                )
                for item in range(count * planes)
            ],
            axis=0,
        ).astype(BF16)
        bent.append(fold(dot(pair, to_ref[...]), 1))
    for bit in range(PARTS):
        for item in range(count * planes):
            band, plane = divmod(item, planes)
            for part in range(2):
                found_ref[bit, pl.ds((2 * band + part) * planes + plane, USED, stride=rows), :] = bent[bit][
                    item * STEP : item * STEP + USED, lanes(part)
                ]
    for bit in range(PARTS):
        field_ref[:, lanes(bit)] = found_ref[bit].astype(BF16)
    for owner in range(owners):
        here = slice(owner * cols, (owner + 1) * cols)
        values = dot(field_ref[...], pick_ref[:, here])
        first = jnp.broadcast_to(first_ref[owner : owner + 1, :], (rows, cols))
        zero = jnp.zeros((rows, cols), F32)
        total = zero
        for at in range(USED):
            total += jnp.where(first == at, values[at * rows : (at + 1) * rows], zero)
        out_ref[owner] = total.astype(BF16)


def on_grid(waves, potential):
    owners, rows, cols = waves.shape
    rows -= 8
    pieces = [jnp.asarray(tables(owners)[name]) for name in ("two_in", "one_in", "one_out", "two_out")]
    return pl.pallas_call(
        grid_kernel,
        in_specs=[whole(*waves.shape), whole(*potential.shape)] + [whole(*piece.shape) for piece in pieces],
        out_specs=whole(owners, rows, cols),
        out_shape=jax.ShapeDtypeStruct((owners, rows, cols), BF16),
        scratch_shapes=[
            pltpu.VMEM((PARTS * LEN, owners * cols), BF16),
            pltpu.VMEM((owners, cols), jnp.int32),
            pltpu.VMEM((rows * STEP, owners * cols), BF16),
            pltpu.VMEM((PARTS, rows * USED, LEN), F32),
            pltpu.VMEM((rows * USED, PARTS * LEN), BF16),
        ],
        compiler_params=pltpu.CompilerParams(vmem_limit_bytes=56 << 20),
        cost_estimate=pl.CostEstimate(
            flops=2 * 2 * rows * USED * PARTS * LEN * owners * cols,
            bytes_accessed=4 << 20,
            transcendentals=0,
        ),
        name="on_grid",
    )(waves, potential, *pieces)


def collect_kernel(slot_ref, cols_ref, panel_ref, in_ref, table_ref, out_ref, wide_ref, held_ref):
    owners, rows, cols = in_ref.shape
    count = panel_ref.shape[0]
    tall = rows // count
    base = 2 * count * THIRDS

    @pl.when(pl.program_id(0) == 0)
    def _():
        for band in range(count):
            waves = in_ref[:, band * tall : (band + 1) * tall, :].reshape(owners * tall, cols)
            found = fold(dot(table_ref[...], waves), 0)
            for part in range(2):
                for at in range(cols // LEN):
                    wide_ref[at, pl.ds(part * count + band, THIRDS, stride=2 * count), :] = found[
                        part * THIRDS : (part + 1) * THIRDS, at * LEN : (at + 1) * LEN
                    ]
        for at in range(cols // LEN):
            high, low = halves(wide_ref[at])
            held_ref[:base, at * LEN : (at + 1) * LEN] = high
            held_ref[:base, cols + at * LEN : cols + (at + 1) * LEN] = low
        column = cols_ref[...]
        first = column >> 7
        second = column & (LEN - 1)
        first = jnp.where(first < LEN // 2, first, first - LEN)
        second = jnp.where(second < LEN // 2, second, second - LEN)
        size = first * first + second * second
        line = lax.broadcasted_iota(jnp.int32, (16, cols), 0)
        size = jnp.where(line == 0, size >> 7, jnp.where(line == 1, size & (LEN - 1), 0))
        held_ref[base:, :cols] = size.astype(F32).astype(BF16)
        held_ref[base:, cols:] = jnp.zeros((16, cols), BF16)

    slot = slot_ref[...]
    pick = one_hot(slot >> 7, cols).astype(BF16)
    third = third_slot(slot)
    found = dot(held_ref[...], jnp.concatenate([pick, pick], axis=0))
    panel = jnp.concatenate([panel_ref[:, part, :] for part in range(2)], axis=0)
    where = jnp.broadcast_to(third, panel.shape)
    zero = jnp.zeros_like(panel)
    tall = 2 * count
    back = [zero] * 4
    for index in range(THIRDS):
        back[index % 4] += jnp.where(where == index, found[index * tall : (index + 1) * tall], zero)
    third = (third - HALF_THREE).astype(F32)
    kinetic = (float(LEN) * found[base : base + 1] + found[base + 1 : base + 2] + third * third) * (
        2.0 / LEN**2
    )
    out_ref[...] = (kinetic * panel + ((back[0] + back[1]) + (back[2] + back[3]))).astype(BF16)


def collect(panel, slot, columns, waves, start, length, chunk):
    count = panel.shape[0]
    owners, rows, cols = waves.shape
    table = tables(owners)["three_out"]
    skip = start // chunk
    return pl.pallas_call(
        collect_kernel,
        grid=(length // chunk,),
        in_specs=[
            pl.BlockSpec((1, chunk), lambda i: (0, i + skip)),
            whole(1, cols),
            pl.BlockSpec((count, 2, chunk), lambda i: (0, 0, i + skip)),
            whole(*waves.shape),
            whole(*table.shape),
        ],
        out_specs=pl.BlockSpec((2 * count, chunk), lambda i: (0, i)),
        out_shape=jax.ShapeDtypeStruct((2 * count, length), BF16),
        scratch_shapes=[
            pltpu.VMEM((cols // LEN, 2 * count * THIRDS, LEN), F32),
            pltpu.VMEM((2 * count * THIRDS + 16, 2 * cols), BF16),
        ],
        compiler_params=pltpu.CompilerParams(vmem_limit_bytes=40 << 20),
        cost_estimate=pl.CostEstimate(
            flops=2 * 4 * count * THIRDS * cols * length, bytes_accessed=4 << 20, transcendentals=0
        ),
        name="collect",
    )(slot, columns, panel, waves, jnp.asarray(table))


def project_kernel(sizes, seat_ref, *refs):
    pieces, (both_ref, prev_ref, out_ref, acc_ref) = refs[: len(sizes)], refs[len(sizes) :]
    step = pl.program_id(0)

    @pl.when(step == 0)
    def _():
        acc_ref[...] = jnp.zeros_like(acc_ref)

    rows = jnp.concatenate([ref[...].reshape(-1, ref.shape[-1]) for ref in pieces], axis=0)
    acc_ref[...] += dot_nt(rows, both_ref[...])

    @pl.when(step == pl.num_programs(0) - 1)
    def _():
        half = acc_ref.shape[1] // 2
        out_ref[...] = prev_ref[...]
        blocks = []
        for piece in range(acc_ref.shape[0] // 8):
            real = acc_ref[8 * piece : 8 * piece + 4]
            imag = acc_ref[8 * piece + 4 : 8 * piece + 8]
            blocks.append((real[:, :half] + imag[:, half:], imag[:, :half] - real[:, half:]))
        for pair in range(len(blocks) // 2):
            odd = seat_ref[8] == 1
            for part in range(2):
                one, two = blocks[2 * pair][part], blocks[2 * pair + 1][part]
                tile = jnp.concatenate([jnp.where(odd, two, one), jnp.where(odd, one, two)], axis=0)
                seat = seat_ref[pair] + part * (len(blocks) // 2)
                out_ref[seat] = out_ref[seat] + tile


def project(pieces, both, prev, seats, start, chunk):
    length = pieces[0].shape[-1]
    sizes = [math.prod(piece.shape[:-1]) for piece in pieces]
    skip = start // chunk
    block = lambda piece: pl.BlockSpec(
        piece.shape[:-1] + (chunk,), lambda i, *_, n=piece.ndim: (0,) * (n - 1) + (i,)
    )
    return pl.pallas_call(
        functools.partial(project_kernel, sizes),
        grid_spec=pltpu.PrefetchScalarGridSpec(
            num_scalar_prefetch=1,
            grid=(length // chunk,),
            in_specs=[block(piece) for piece in pieces]
            + [
                pl.BlockSpec((both.shape[0], chunk), lambda i, *_: (0, i + skip)),
                whole(*prev.shape),
            ],
            out_specs=whole(*prev.shape),
            scratch_shapes=[pltpu.VMEM((sum(sizes), both.shape[0]), F32)],
        ),
        out_shape=jax.ShapeDtypeStruct(prev.shape, F32),
        compiler_params=pltpu.CompilerParams(vmem_limit_bytes=32 << 20),
        cost_estimate=pl.CostEstimate(
            flops=2 * 256 * both.shape[0] * length,
            bytes_accessed=2 * both.shape[0] * length,
            transcendentals=0,
        ),
        name="project",
    )(seats, *pieces, both, prev)


def moved(x, axis, target):
    size = lax.axis_size(axis)
    return lax.ppermute(x, axis, [(i, target(i) % size) for i in range(size)])


def share(x, meanwhile):
    pair = jnp.stack([x, moved(x, "band", lambda i: i ^ 1)])
    pair, meanwhile = lax.optimization_barrier((pair, meanwhile))
    below = moved(pair, "band", lambda i: i + 2)
    above = moved(pair, "band", lambda i: i - 2)
    far = [moved(below[0], "band", lambda i: i + 2), moved(above[1], "band", lambda i: i - 2)]
    return [pair, below, above] + far, meanwhile


def per_device(slab, panel, potential, pw_slot, columns):
    parts = lax.axis_size("pw")
    bands, _, length = slab.shape
    cols = columns.shape[0]
    slot = pw_slot.reshape(1, length)
    columns = columns.reshape(1, cols)
    waves, coeffs = spread(panel, slot, columns, parts, 3072)
    waves = lax.all_to_all(waves, "pw", split_axis=0, concat_axis=0, tiled=True)
    coeffs = lax.all_gather(coeffs, "band", axis=0, tiled=True)
    both = jnp.transpose(slab, (1, 0, 2)).reshape(2 * bands, length)
    waves, both = lax.optimization_barrier((waves, both))
    waves = on_grid(waves, potential)
    waves = lax.all_to_all(waves, "pw", split_axis=0, concat_axis=0, tiled=True)
    waves, coeffs = lax.optimization_barrier((waves, coeffs))
    me = lax.axis_index("band")
    row, odd = me // 2, me % 2
    terms = jnp.zeros((parts, bands // parts, bands), F32)
    pick = lambda *seats: jnp.stack([jnp.asarray(seat, jnp.int32) for seat in seats])
    applied = collect(panel, slot, columns, waves, 0, length, 3072)
    seats = pick(8, 9, 10, 11, 0, 0, 0, 0, 0)
    terms = project([coeffs], both, terms, seats, 0, 3072)
    shared, terms = share(applied, terms)
    seats = pick(row, (row + 3) % 4, (row + 1) % 4, (row + 2) % 4, 0, 0, 0, 0, odd)
    terms = project(shared, both, terms, seats, 0, 3072)
    terms = lax.all_to_all(terms, "pw", split_axis=0, concat_axis=0, tiled=True)
    return jnp.sum(terms, axis=0).T


def solution(mesh):
    in_specs = (P("band", None, "pw"), P("band", None, "pw"), P("pw", None, None), P("pw"), P("pw"))
    out_specs = P("band", "pw")
    return jax.shard_map(
        per_device, mesh=mesh, in_specs=in_specs, out_specs=out_specs, check_vma=False
    )
```
